256 devices in a mesh: prompt: 8 (over y, x_lo), sample: 4 (over x_hi, core), expert: 8 (over z).
Axes of the slice: x: 4 (x_hi: 2, x_lo: 2; x = x_hi * 2 + x_lo), y: 4, z: 8, core: 2. Of those that a mesh axis runs over, the one named last changes fastest.
Arguments:
- residual: bfloat16 [8192, 2880], P(('prompt', 'sample')), may hold values from -16 to 16
- queries: bfloat16 [8192, 4096], P(('prompt', 'sample'), 'expert'), may hold values from -6 to 6
- response_key_value: bfloat16 [8192, 8, 128], P(('prompt', 'sample'), 'expert'), may hold values from -8 to 8
- prompt_cache: bfloat16 [8, 8192, 8, 128], P('prompt', 'sample', 'expert'), may hold values from -6 to 6
- lengths: int32 [32], P(('prompt', 'sample')), may hold values from 32 to 256
- out_proj: bfloat16 [4096, 2880], P('expert'), may hold values from -0.75 to 0.75
- norm_gain: float32 [2880], replicated, may hold values from 0.25 to 1.75
- gate_up: bfloat16 [64, 2880, 2880], P(('prompt', 'sample'), None, 'expert'), may hold values from -0.109375 to 0.109375
- down_proj: bfloat16 [64, 1440, 2880], P(('prompt', 'sample'), 'expert'), may hold values from -0.15625 to 0.15625
- expert_ids: int32 [8192, 4], P(('prompt', 'sample')), may hold values from 0 to 63, all different within a row; in each aligned block of 256 rows (0 to 255, 256 to 511, ...) at most 20 rows name the same one
- gate_weights: float32 [8192, 4], P(('prompt', 'sample')), may hold values from 0.1 to 0.5
Outputs:
- scored: bfloat16 [8192, 2880], P(('prompt', 'sample', 'expert'))
The draws below stay inside these ranges and needn't reach their ends.
Inputs may be any that keep to these rules, and one draw needn't show every extreme that they name: `expert_ids`: among the 256 tokens of one sample no expert is named more than 20 times, and in some sample some expert is named exactly 20 times.
All inputs are finite; a program needn't handle non-finite values.
Results may differ from the reference program's by a relative error of at most 0.017.
Values may be sent and summed in bfloat16 or wider, within the bound.
No kernel may reach another device: no remote copies, remote signals or barrier semaphores. Data moves between devices by JAX's collectives and lax.ppermute only.
A program may use at most 128 MiB of HBM per device.

```python
import math
import jax
import jax.numpy as jnp
import numpy as np
from jax import lax

D = 2880
QUERY_HEADS = 64
KEY_VALUE_HEADS = 8
HEAD_SIZE = 64
TOPK = 4
FF = 1440
RESPONSE_LENGTH = 256
E = 64
PROMPT_LENGTH = 8192
PROMPT_TOTAL = 8
SAMPLE_GROUPS = 32
TOKEN_TOTAL = 8192
CAP = 20
N_SAMPLE = 4
N_EXPERT = 8


def draw_queries(key, part):
    key = jax.random.fold_in(key, 1)
    values = jnp.clip(jax.random.normal(key, (TOKEN_TOTAL, QUERY_HEADS, HEAD_SIZE), jnp.float32), -6.0, 6.0)
    return values.reshape(TOKEN_TOTAL, QUERY_HEADS * HEAD_SIZE).astype(jnp.bfloat16)


def draw_prompt_cache(key, part):
    key = jax.random.fold_in(key, 2)
    key_keys, key_values = jax.random.split(key)
    array_shape = (PROMPT_TOTAL, PROMPT_LENGTH, KEY_VALUE_HEADS, HEAD_SIZE)
    keys_part = jnp.clip(1.5 * jax.random.normal(key_keys, array_shape, jnp.float32), -6.0, 6.0)
    values_part = jnp.clip(jax.random.normal(key_values, array_shape, jnp.float32), -6.0, 6.0)
    return jnp.concatenate([keys_part, values_part], axis=-1).astype(jnp.bfloat16)


def draw_response_key_value(key, part):
    key = jax.random.fold_in(key, 3)
    key_keys, key_values = jax.random.split(key)
    array_shape = (TOKEN_TOTAL, KEY_VALUE_HEADS, HEAD_SIZE)
    keys_part = jnp.clip(2.5 * jax.random.normal(key_keys, array_shape, jnp.float32), -8.0, 8.0)
    values_part = jnp.clip(jax.random.normal(key_values, array_shape, jnp.float32), -6.0, 6.0)
    return jnp.concatenate([keys_part, values_part], axis=-1).astype(jnp.bfloat16)


def draw_residual(key, part):
    key = jax.random.fold_in(key, 4)
    key_base = jax.random.fold_in(key, 0)
    values = jnp.clip(jax.random.normal(key_base, (TOKEN_TOTAL, D), jnp.float32), -6.0, 6.0)
    return values.astype(jnp.bfloat16)


def plant(entries, rng, least, high):
    longest = entries.shape.index(max(entries.shape))
    spots = []
    for shift in (0, 1):
        where = [jax.random.randint(jax.random.fold_in(rng, axis), (), 0, length) for axis, length in enumerate(entries.shape)]
        where[longest] = (where[longest] + shift) % entries.shape[longest]
        spots.append(tuple(where))
    return entries.at[spots[0]].set(least).at[spots[1]].set(high)


def block_levels(key, dims, cuts, least, top_value):
    def one(dim, blocks):
        steps = jax.random.uniform(jax.random.fold_in(jax.random.fold_in(key, 6), dim), (blocks,), jnp.float32, least / len(cuts), top_value / len(cuts))
        return jnp.repeat(jnp.exp(steps), dims[dim] // blocks).reshape((-1,) + (1,) * (len(dims) - dim - 1))

    level = one(*cuts[0])
    for cut in cuts[1:]:
        level = level * one(*cut)
    return level


def deal_out(key, own, number, rows, amount, top, most, lean):
    sequence = jax.random.permutation(key, amount)
    heavy_load, ordinary = shares(amount, rows * top, most, lean, True), shares(amount, rows * top, most, lean, False)
    places = jnp.arange(amount)

    def named(sizes, turn):
        used = int((sizes > 0).sum())
        fixed = max(1, used // 4)
        passed = fixed + (places - fixed + turn * (used - fixed)) % max(1, amount - fixed)
        return jnp.zeros((amount,), jnp.int32).at[sequence[jnp.where(places < fixed, places, passed)]].set(jnp.asarray(sizes, jnp.int32))

    sizes = jnp.where(number % 4 == 0, named(heavy_load, number // 4), named(ordinary, number - number // 4 - 1))
    mixed = jax.random.permutation(jax.random.fold_in(own, 3), amount)
    donor, receiver = mixed[0:amount // 2 * 2:2], mixed[1:amount // 2 * 2:2]
    slack = jnp.minimum(sizes[donor] - 1, most - sizes[receiver]) // 2
    slack = jnp.where((donor == sequence[0]) | (receiver == sequence[0]) | (sizes[receiver] == 0), 0, jnp.maximum(slack, 0))
    passed = jax.random.randint(jax.random.fold_in(own, 4), (amount // 2,), 0, 1 << 20) % (slack + 1)
    sizes = sizes.at[donor].add(-passed).at[receiver].add(passed)
    labels = jnp.searchsorted(jnp.cumsum(sizes), jnp.arange(rows * top), side="right").astype(jnp.int32)
    table = labels.reshape(top, rows).T
    table = table[jax.random.permutation(jax.random.fold_in(own, 1), rows)]
    turn = jax.random.randint(jax.random.fold_in(own, 2), (rows, 1), 0, top)
    return jnp.take_along_axis(table, (jnp.arange(top)[None, :] + turn) % top, axis=1)


def shares(number_of, total, reach, slope, full):
    weights = [(1 << 20) // math.isqrt(grade ** slope) + 1 for grade in range(1, number_of + 1)]
    largest = reach if full else min(reach, max(-(-total // number_of), total * weights[0] // sum(weights)))
    least = 1 if total - largest >= number_of - 1 else 0
    counts, rest = [largest] + [least] * (number_of - 1), total - largest - least * (number_of - 1)
    while rest > 0:
        candidates = [i for i in range(1, number_of) if counts[i] < largest] or [i for i in range(1, number_of) if counts[i] < reach]
        mass, budget = sum([weights[i] for i in candidates]), rest
        for i in candidates:
            addition = min(reach - counts[i], max(1, budget * weights[i] // mass), rest)
            counts[i] = counts[i] + addition
            rest = rest - addition
    return np.array(counts)


def noise(rng, shape, deviation, bound, pieces=(), held_as=jnp.bfloat16):
    values = jax.random.normal(rng, shape, jnp.float32) * deviation
    if len(pieces) > 0:
        values = block_levels(rng, shape, pieces, -0.22, 0.18) * values
    return jnp.clip(values, min=-bound, max=bound).astype(held_as)


def setup_inputs(seed: int = 0) -> dict:
    key_of = jax.random.split(jax.random.key(seed), 12)
    residual = draw_residual(jax.random.fold_in(key_of[11], 71), 0)
    queries = draw_queries(jax.random.fold_in(key_of[11], 71), 0)
    response_key_value = draw_response_key_value(jax.random.fold_in(key_of[11], 71), 0)
    prompt_cache = draw_prompt_cache(jax.random.fold_in(key_of[11], 71), 0)
    lengths = plant(jax.random.randint(key_of[4], (SAMPLE_GROUPS,), RESPONSE_LENGTH // 8, RESPONSE_LENGTH + 1), jax.random.fold_in(key_of[4], 1), RESPONSE_LENGTH // 8, RESPONSE_LENGTH).astype(jnp.int32)
    out_proj = noise(key_of[5], (QUERY_HEADS * HEAD_SIZE, D), HEAD_SIZE ** -0.5, 0.75, ((0, 8),))
    norm_gain = jnp.clip(1.0 + 0.15 * jax.random.normal(key_of[6], (D,), jnp.float32), 0.25, 1.75)
    gate_up = noise(key_of[7], (E, D, 2 * FF), D ** -0.5, 0.109375, ((0, 32), (2, 8)))
    down_proj = noise(key_of[8], (E, FF, D), FF ** -0.5, 0.15625, ((0, 32), (1, 8)))
    expert_ids_keys = jax.random.split(jax.random.fold_in(key_of[9], 1), TOKEN_TOTAL // RESPONSE_LENGTH)
    expert_ids_turns = jax.random.permutation(jax.random.fold_in(key_of[9], 3), TOKEN_TOTAL // RESPONSE_LENGTH)
    expert_ids = jax.vmap(lambda own, number: deal_out(jax.random.fold_in(key_of[9], 2), own, number, RESPONSE_LENGTH, E, TOPK, CAP, 1))(expert_ids_keys, expert_ids_turns).reshape((TOKEN_TOTAL, TOPK))
    gate_weights = jnp.clip(0.1 + 0.4 * jax.random.uniform(key_of[10], (TOKEN_TOTAL, TOPK), jnp.float32) ** block_levels(key_of[10], (TOKEN_TOTAL, TOPK), ((0, 32),), -0.2, 0.2), 0.1, 0.5)
    return dict(residual=residual, queries=queries, response_key_value=response_key_value, prompt_cache=prompt_cache, lengths=lengths, out_proj=out_proj, norm_gain=norm_gain, gate_up=gate_up, down_proj=down_proj, expert_ids=expert_ids, gate_weights=gate_weights)


def head_attention(operands):
    queries_by_head, keys_by_head, head_values, allowed = operands
    scores = jnp.einsum('rgd,kd->grk', queries_by_head, keys_by_head) * HEAD_SIZE ** (-0.5)
    scores = jnp.where(allowed[None], scores, -1e+30)
    row_max = lax.optimization_barrier(jnp.max(scores, axis=-1, keepdims=True))
    raised = jnp.exp(scores - row_max)
    denominator = lax.optimization_barrier(jnp.sum(raised, axis=-1))
    probs = lax.optimization_barrier(raised.astype(jnp.bfloat16)).astype(jnp.float32)
    return jnp.einsum('grk,kd->grd', probs, head_values) / denominator[..., None]

def group_core(queries_by_group, group_kv, group_length, cache):
    row_pos = lax.broadcasted_iota(jnp.int32, (RESPONSE_LENGTH, RESPONSE_LENGTH), 0)
    col_pos = lax.broadcasted_iota(jnp.int32, (RESPONSE_LENGTH, RESPONSE_LENGTH), 1)
    resp_allowed = (col_pos <= row_pos) & (col_pos < group_length)
    allowed = jnp.concatenate([jnp.ones((RESPONSE_LENGTH, PROMPT_LENGTH), bool), resp_allowed], axis=1)
    all_keys = jnp.concatenate([cache[:, :, :HEAD_SIZE], group_kv[:, :, :HEAD_SIZE]], axis=0).astype(jnp.float32)
    all_values = jnp.concatenate([cache[:, :, HEAD_SIZE:], group_kv[:, :, HEAD_SIZE:]], axis=0).astype(jnp.float32)
    reshaped_array = queries_by_group.reshape(RESPONSE_LENGTH, KEY_VALUE_HEADS, QUERY_HEADS // KEY_VALUE_HEADS, HEAD_SIZE).astype(jnp.float32)
    head_out = lax.map(lambda ops: head_attention((ops[0], ops[1], ops[2], allowed)), (reshaped_array.transpose(1, 0, 2, 3), all_keys.transpose(1, 0, 2), all_values.transpose(1, 0, 2)))
    return head_out.transpose(2, 0, 1, 3).reshape(RESPONSE_LENGTH, QUERY_HEADS * HEAD_SIZE).astype(jnp.bfloat16)

def fill_tables(slot_row, gate_row):
    token_of = jnp.zeros((E * CAP,), jnp.int32).at[slot_row].set(jnp.arange(RESPONSE_LENGTH * TOPK, dtype=jnp.int32) // TOPK)
    weight_of = jnp.zeros((E * CAP,), jnp.float32).at[slot_row].set(gate_row)
    return (token_of, weight_of)

def reference(residual, queries, response_key_value, prompt_cache, lengths, out_proj, norm_gain, gate_up, down_proj, expert_ids, gate_weights):

    def rows_per_group(operands):
        queries_by_group, group_kv, group_length, group_index = operands
        cache = lax.dynamic_index_in_dim(prompt_cache, (group_index // N_SAMPLE).astype(jnp.int32), 0, keepdims=False)
        return group_core(queries_by_group, group_kv, group_length, cache)
    attention_result = lax.map(rows_per_group, (queries.reshape(SAMPLE_GROUPS, RESPONSE_LENGTH, QUERY_HEADS * HEAD_SIZE), response_key_value.reshape(SAMPLE_GROUPS, RESPONSE_LENGTH, KEY_VALUE_HEADS, 2 * HEAD_SIZE), lengths.astype(jnp.int32), jnp.arange(SAMPLE_GROUPS, dtype=jnp.int32)))
    attention_result = attention_result.reshape(TOKEN_TOTAL, QUERY_HEADS * HEAD_SIZE)
    projected = jnp.dot(attention_result, out_proj, preferred_element_type=jnp.float32)
    hidden_state = residual.astype(jnp.float32) + projected
    inverse = lax.rsqrt(lax.optimization_barrier(jnp.mean(hidden_state * hidden_state, axis=-1, keepdims=True)) + 1e-05)
    normed = (hidden_state * inverse * norm_gain).astype(jnp.bfloat16)
    flat_ids = expert_ids.reshape(SAMPLE_GROUPS, RESPONSE_LENGTH * TOPK).astype(jnp.int32)
    one_hot = (flat_ids[..., None] == jnp.arange(E, dtype=jnp.int32)).astype(jnp.int32)
    earlier = jnp.cumsum(one_hot, axis=1) - one_hot
    position = lax.optimization_barrier(jnp.sum(earlier * one_hot, axis=-1)).astype(jnp.int32)
    slot_index = flat_ids * CAP + position
    token_of, weight_of = jax.vmap(fill_tables)(slot_index, gate_weights.reshape(SAMPLE_GROUPS, RESPONSE_LENGTH * TOPK))
    normed_groups = normed.reshape(SAMPLE_GROUPS, RESPONSE_LENGTH, D)
    group_rows = jnp.arange(SAMPLE_GROUPS, dtype=jnp.int32)[:, None]

    def one_expert(mixture, expert_index):
        token_idx = lax.dynamic_slice_in_dim(token_of, expert_index * CAP, CAP, 1)
        slot_weight = lax.dynamic_slice_in_dim(weight_of, expert_index * CAP, CAP, 1)
        picked_rows = jnp.take_along_axis(normed_groups, token_idx[..., None], axis=1).reshape(SAMPLE_GROUPS * CAP, D)
        both = jnp.dot(picked_rows, lax.dynamic_index_in_dim(gate_up, expert_index, 0, keepdims=False), preferred_element_type=jnp.float32)
        gate_part = both[:, 0::2]
        up_part = both[:, 1::2]
        activation = ((up_part + 1.0) * gate_part * jax.nn.sigmoid(1.702 * gate_part)).astype(jnp.bfloat16)
        block_input = activation.reshape(SAMPLE_GROUPS * CAP, N_EXPERT, FF // N_EXPERT).astype(jnp.float32)
        down_weight_blocks = lax.dynamic_index_in_dim(down_proj, expert_index, 0, keepdims=False).reshape(N_EXPERT, FF // N_EXPERT, D).astype(jnp.float32)
        block_output = jnp.einsum('lkr,krn->lkn', block_input, down_weight_blocks)
        block_output = lax.optimization_barrier(block_output.astype(jnp.bfloat16)).astype(jnp.float32)
        expert_out = lax.optimization_barrier(jnp.sum(block_output, axis=1)) * slot_weight.reshape(SAMPLE_GROUPS * CAP)[:, None]
        mixture = mixture.at[group_rows, token_idx].add(expert_out.reshape(SAMPLE_GROUPS, CAP, D))
        return (mixture, None)
    mixture, _ = lax.scan(one_expert, jnp.zeros((SAMPLE_GROUPS, RESPONSE_LENGTH, D), jnp.float32), jnp.arange(E, dtype=jnp.int32))
    return (hidden_state + mixture.reshape(TOKEN_TOTAL, D)).astype(jnp.bfloat16)
```

```python
import functools
import math

import jax
import jax.numpy as jnp
import numpy as np
from jax import lax
from jax.experimental import pallas as pl
from jax.experimental.pallas import tpu as pltpu
from jax.sharding import Mesh, PartitionSpec as P

F32 = jnp.float32
BF16 = jnp.bfloat16
ROWS = 256
CHUNK = 32
WIDTH = 2880
HEAD = 64
CAP = 20
PAD_CAP = 24
CHIPS = 16
SLOTS = CHIPS * PAD_CAP
KEY_BLOCK = 1024
VMEM_LIMIT = 48 * 1024 * 1024
COLUMN_CUTS = ((0, 768), (768, 1536), (1536, 2304), (2304, 2880))


def params(count=0):
    if count:
        return pltpu.CompilerParams(
            vmem_limit_bytes=VMEM_LIMIT, dimension_semantics=("arbitrary",) * count
        )
    return pltpu.CompilerParams(vmem_limit_bytes=VMEM_LIMIT)


def whole(shape):
    return pl.BlockSpec(shape, lambda *_: (0,) * len(shape))


def spread_cache(kv, keys_ref, even_ref, odd_ref, start):
    rows = kv.shape[0]
    wide = kv.astype(F32)
    turned = pltpu.roll(wide, HEAD, 1)
    first = lax.broadcasted_iota(jnp.int32, wide.shape, 1) < HEAD
    keys_ref[pl.ds(start, rows), :] = jnp.where(first, wide, turned).astype(BF16)
    even_ref[pl.ds(start, rows), :] = jnp.where(first, turned, 1.0).astype(BF16)
    odd_ref[pl.ds(start, rows), :] = jnp.where(first, 1.0, wide).astype(BF16)


def spread_queries(block):
    scaled = block.astype(F32) * (HEAD ** -0.5 * math.log2(math.e))
    high = scaled.astype(BF16).astype(F32)
    low = scaled - high
    first = lax.broadcasted_iota(jnp.int32, scaled.shape, 1) < HEAD
    even = jnp.where(first, high, pltpu.roll(low, HEAD, 1)).astype(BF16)
    odd = jnp.where(first, pltpu.roll(high, HEAD, 1), low).astype(BF16)
    return even, odd


def scores_of(queries, keys):
    return lax.dot_general(
        queries, keys, (((1,), (1,)), ((), ())), preferred_element_type=F32
    )


def attend(queries, keys_ref, values_ref, cuts, top, total, allowed):
    for start, size in cuts:
        scores = scores_of(queries, keys_ref[start : start + size, :])
        if allowed is not None and start == 0:
            scores = jnp.where(allowed, scores, -1e30)
        block_top = jnp.max(scores, axis=1, keepdims=True)
        new_top = block_top if top is None else jnp.maximum(top, block_top)
        raised = jnp.exp2(scores - new_top).astype(BF16)
        part = jnp.dot(raised, values_ref[start : start + size, :], preferred_element_type=F32)
        total = part if top is None else total * jnp.exp2(top - new_top) + part
        top = new_top
    return top, total


def first_kernel(
    length_ref, q_ref, resp_ref, own_ref, near_ref, top_ref, total_ref, keys, even, odd
):
    piece = own_ref.shape[0]

    @pl.when(pl.program_id(0) == 0)
    def _():
        spread_cache(resp_ref[...], keys, even, odd, 0)
        spread_cache(own_ref[...], keys, even, odd, ROWS)
        spread_cache(near_ref[...], keys, even, odd, ROWS + piece)

    row = lax.broadcasted_iota(jnp.int32, (ROWS, ROWS), 0)
    col = lax.broadcasted_iota(jnp.int32, (ROWS, ROWS), 1)
    allowed = (col <= row) & (col < length_ref[0])
    cuts = [(0, ROWS)] + [
        (ROWS + start, KEY_BLOCK) for start in range(0, 2 * piece, KEY_BLOCK)
    ]
    pair = spread_queries(q_ref[...])
    for side, values in enumerate((even, odd)):
        top, total = attend(pair[side], keys, values, cuts, None, None, allowed)
        top_ref[side] = jnp.broadcast_to(top, (ROWS, 2 * HEAD))
        total_ref[side] = total


def second_kernel(
    place_ref, q_ref, a_ref, b_ref, top_ref, total_ref, proj_ref, *rest
):
    outs, (keys, even, odd, attended, turned) = rest[:8], rest[8:]
    piece = a_ref.shape[0]
    step = pl.program_id(0)

    @pl.when(step == 0)
    def _():
        spread_cache(a_ref[...], keys, even, odd, 0)
        spread_cache(b_ref[...], keys, even, odd, piece)

    cuts = [(start, KEY_BLOCK) for start in range(0, 2 * piece, KEY_BLOCK)]
    pair = spread_queries(q_ref[...])
    totals = []
    for side, values in enumerate((even, odd)):
        _, total = attend(
            pair[side], keys, values, cuts, top_ref[side][:, :1], total_ref[side], None
        )
        totals.append(total)
    first = lax.broadcasted_iota(jnp.int32, (ROWS, 2 * HEAD), 1) < HEAD
    numerator = jnp.where(first, totals[0], totals[1])
    denominator = jnp.where(
        first, pltpu.roll(totals[0], HEAD, 1), pltpu.roll(totals[1], HEAD, 1)
    )
    attended[step] = (numerator / denominator).astype(BF16)

    @pl.when(step == pl.num_programs(0) - 1)
    def _():
        for k in range(8):
            source = pl.multiple_of(lax.rem(place_ref[0] + k, 8) * CHUNK, CHUNK)
            for j in range(4):
                turned[CHUNK * k : CHUNK * (k + 1), 128 * j : 128 * (j + 1)] = attended[
                    j, pl.ds(source, CHUNK), :
                ]
        rows = turned[...]
        for low, high in COLUMN_CUTS:
            part = jnp.dot(rows, proj_ref[:, low:high], preferred_element_type=F32).astype(BF16)
            for k in range(8):
                outs[k][:, low:high] = part[CHUNK * k : CHUNK * (k + 1)]


def attention(place, lengths, queries, response, own, near, far, far_near, out_proj):
    pairs = queries.shape[1] // (2 * HEAD)
    piece = own.shape[0]
    state = (2 * pairs, ROWS, 2 * HEAD)
    state_spec = pl.BlockSpec((2, ROWS, 2 * HEAD), lambda i: (i, 0, 0))
    query_spec = pl.BlockSpec((ROWS, 2 * HEAD), lambda i: (0, i))
    smem = pl.BlockSpec(memory_space=pltpu.SMEM)

    def spread(rows):
        return [pltpu.VMEM((rows, 2 * HEAD), BF16)] * 3

    flops = 8 * ROWS * 4 * 2 * HEAD * 2 * piece
    cost = pl.CostEstimate(
        flops=flops, bytes_accessed=5 << 20, transcendentals=8 * ROWS * 2 * piece
    )
    top, total = pl.pallas_call(
        first_kernel,
        grid=(pairs,),
        in_specs=[
            smem,
            query_spec,
            whole((ROWS, 2 * HEAD)),
            whole((piece, 2 * HEAD)),
            whole((piece, 2 * HEAD)),
        ],
        out_specs=[state_spec, state_spec],
        out_shape=[jax.ShapeDtypeStruct(state, F32)] * 2,
        scratch_shapes=spread(ROWS + 2 * piece),
        compiler_params=params(1),
        cost_estimate=cost,
        name="attend_near",
    )(lengths, queries, response, own, near)
    return pl.pallas_call(
        second_kernel,
        grid=(pairs,),
        in_specs=[
            smem,
            query_spec,
            whole((piece, 2 * HEAD)),
            whole((piece, 2 * HEAD)),
            state_spec,
            state_spec,
            whole(out_proj.shape),
        ],
        out_specs=[whole((CHUNK, WIDTH))] * 8,
        out_shape=[jax.ShapeDtypeStruct((CHUNK, WIDTH), BF16)] * 8,
        scratch_shapes=spread(2 * piece)
        + [pltpu.VMEM((pairs, ROWS, 2 * HEAD), BF16), pltpu.VMEM((ROWS, queries.shape[1]), BF16)],
        compiler_params=params(1),
        cost_estimate=cost,
        name="attend_far",
    )(place, queries, far, far_near, top, total, out_proj)


def routing_kernel(place_ref, ids_ref, weights_ref, send_ref, mix_ref):
    ids = ids_ref[...]
    weights = weights_ref[...]
    routes = ids.shape[1]
    expert = lax.broadcasted_iota(jnp.int32, (ROWS, 128), 1)
    named = [ids[:, r : r + 1] == expert for r in range(routes)]
    count = sum(jnp.where(n, 1.0, 0.0) for n in named)
    row = lax.broadcasted_iota(jnp.int32, (ROWS, ROWS), 0)
    col = lax.broadcasted_iota(jnp.int32, (ROWS, ROWS), 1)
    earlier = jnp.dot(
        jnp.where(col < row, 1.0, 0.0).astype(BF16),
        count.astype(BF16),
        preferred_element_type=F32,
    )
    slot = lax.broadcasted_iota(jnp.int32, (ROWS, SLOTS), 1)
    group = lax.rem(place_ref[0], 4)
    send = jnp.zeros((ROWS, SLOTS), F32)
    mix = jnp.zeros((ROWS, SLOTS), F32)
    for r in range(routes):
        rank = jnp.sum(jnp.where(named[r], earlier, 0.0), axis=1, keepdims=True)
        chosen = ids[:, r : r + 1]
        chip = lax.shift_right_logical(chosen, 2)
        mine = lax.bitwise_and(chosen, 3) == group
        at = jnp.where(mine, chip * PAD_CAP + rank.astype(jnp.int32), -1)
        hit = slot == at
        send = send + jnp.where(hit, 1.0, 0.0)
        mix = mix + jnp.where(hit, weights[:, r : r + 1], 0.0)
    send_ref[...] = jnp.transpose(send).astype(BF16)
    high = mix.astype(BF16)
    mix_ref[:, :SLOTS] = high
    mix_ref[:, SLOTS:] = (mix - high.astype(F32)).astype(BF16)


def routing(place, ids, weights):
    return pl.pallas_call(
        routing_kernel,
        in_specs=[
            pl.BlockSpec(memory_space=pltpu.SMEM),
            whole(ids.shape),
            whole(weights.shape),
        ],
        grid=(1,),
        out_specs=[whole((SLOTS, ROWS)), whole((ROWS, 2 * SLOTS))],
        out_shape=[
            jax.ShapeDtypeStruct((SLOTS, ROWS), BF16),
            jax.ShapeDtypeStruct((ROWS, 2 * SLOTS), BF16),
        ],
        compiler_params=params(1),
        name="routing",
    )(place, ids, weights)


def norm_kernel(place_ref, residual_ref, gain_ref, *refs):
    parts, (hidden_ref, normed_ref) = refs[:8], refs[8:]
    projected = parts[0][...].astype(F32)
    for part in parts[1:]:
        projected = projected + part[...].astype(F32)
    hidden = residual_ref[...].astype(F32) + projected
    inverse = lax.rsqrt(jnp.mean(hidden * hidden, axis=1, keepdims=True) + 1e-5)
    hidden_ref[...] = hidden
    normed_ref[...] = (hidden * inverse * gain_ref[...]).astype(BF16)


def norm(place, residual, gain, parts):
    chunk = (CHUNK, WIDTH)
    return pl.pallas_call(
        norm_kernel,
        grid_spec=pltpu.PrefetchScalarGridSpec(
            num_scalar_prefetch=1,
            grid=(1,),
            in_specs=[
                pl.BlockSpec(chunk, lambda i, place: (place[0], 0)),
                pl.BlockSpec((1, WIDTH), lambda i, place: (0, 0)),
            ]
            + [pl.BlockSpec(chunk, lambda i, place: (0, 0))] * 8,
            out_specs=[pl.BlockSpec(chunk, lambda i, place: (0, 0))] * 2,
        ),
        out_shape=[jax.ShapeDtypeStruct(chunk, F32), jax.ShapeDtypeStruct(chunk, BF16)],
        compiler_params=params(1),
        name="norm",
    )(place, residual, gain, *parts)


def dispatch_kernel(send_ref, *refs):
    parts, (out_ref, rows) = refs[:8], refs[8:]
    for k in range(8):
        rows[CHUNK * k : CHUNK * (k + 1), :] = parts[k][...]
    for low, high in COLUMN_CUTS:
        out_ref[:, low:high] = jnp.dot(
            send_ref[...], rows[:, low:high], preferred_element_type=F32
        ).astype(BF16)


def dispatch(send, parts):
    return pl.pallas_call(
        dispatch_kernel,
        grid=(1,),
        in_specs=[whole(send.shape)] + [whole((CHUNK, WIDTH))] * 8,
        out_specs=whole((SLOTS, WIDTH)),
        out_shape=jax.ShapeDtypeStruct((SLOTS, WIDTH), BF16),
        scratch_shapes=[pltpu.VMEM((ROWS, WIDTH), BF16)],
        compiler_params=params(1),
        name="dispatch",
    )(send, *parts)


def combine_kernel(mix_ref, back_ref, *outs):
    for low, high in COLUMN_CUTS:
        block = back_ref[:, low:high]
        part = jnp.dot(mix_ref[:, :SLOTS], block, preferred_element_type=F32)
        part = part + jnp.dot(mix_ref[:, SLOTS:], block, preferred_element_type=F32)
        part = part.astype(BF16)
        for k in range(8):
            outs[k][:, low:high] = part[CHUNK * k : CHUNK * (k + 1)]


def combine(mix, back):
    return pl.pallas_call(
        combine_kernel,
        grid=(1,),
        in_specs=[whole(mix.shape), whole(back.shape)],
        out_specs=[whole((CHUNK, WIDTH))] * 8,
        out_shape=[jax.ShapeDtypeStruct((CHUNK, WIDTH), BF16)] * 8,
        compiler_params=params(1),
        name="combine",
    )(mix, back)


def finish_kernel(hidden_ref, *refs):
    parts, out_ref = refs[:8], refs[8]
    total = parts[0][...].astype(F32)
    for part in parts[1:]:
        total = total + part[...].astype(F32)
    out_ref[...] = (hidden_ref[...] + total).astype(BF16)


def finish(hidden, parts):
    return pl.pallas_call(
        finish_kernel,
        grid=(1,),
        in_specs=[whole((CHUNK, WIDTH))] * 9,
        out_specs=whole((CHUNK, WIDTH)),
        out_shape=jax.ShapeDtypeStruct((CHUNK, WIDTH), BF16),
        compiler_params=params(1),
        name="finish",
    )(hidden, *parts)


def expert_kernel(x_ref, *refs):
    ups, downs, (out_ref,) = refs[:2], refs[2:4], refs[4:]
    double, hidden = ups[0].shape[1], downs[0].shape[0]
    rows = x_ref.shape[0]
    lane = lax.broadcasted_iota(jnp.int32, (rows, double), 1)
    even = lax.bitwise_and(lane, 1) == 0
    place = lax.broadcasted_iota(jnp.int32, (double, hidden), 0)
    unit = lax.broadcasted_iota(jnp.int32, (double, hidden), 1)
    spread = jnp.where(place == 2 * unit, 1.0, 0.0).astype(BF16)
    x = x_ref[...]
    acts = []
    for up_ref in ups:
        both = jnp.dot(x, up_ref[...], preferred_element_type=F32)
        up = jnp.concatenate([both[:, 1:], both[:, :1]], axis=1)
        act = (up + 1.0) * both * jax.nn.sigmoid(1.702 * both)
        acts.append(jnp.where(even, act, 0.0).astype(BF16))
    for low, high in COLUMN_CUTS:
        total = None
        for act, down_ref in zip(acts, downs):
            rows_down = jnp.dot(
                spread, down_ref[:, low:high], preferred_element_type=F32
            ).astype(BF16)
            part = jnp.dot(act, rows_down, preferred_element_type=F32)
            total = part if total is None else total + part
        out_ref[:, low:high] = total.astype(out_ref.dtype)


def experts(x, ups, downs, dtype):
    rows = x.shape[0]
    return pl.pallas_call(
        expert_kernel,
        grid=(1,),
        in_specs=[whole(x.shape)] + [whole(w.shape) for w in (*ups, *downs)],
        out_specs=whole((rows, WIDTH)),
        out_shape=jax.ShapeDtypeStruct((rows, WIDTH), dtype),
        compiler_params=params(1),
        cost_estimate=pl.CostEstimate(
            flops=rows * WIDTH * 2160, bytes_accessed=12 << 20, transcendentals=rows * 720
        ),
        name="experts",
    )(x, *ups, *downs)


def weight_plan():
    edges = []
    for group in range(4):
        core = group // 2
        offsets = (0, 1, -1, 2) if group % 2 == 0 else (0, -1, 1, -2)
        for target in (group, group + 4):
            for n, offset in enumerate(offsets):
                source = (core, (target + offset) % 8)
                goal = (core if n < 2 else 1 - core, target)
                edges.append((source, goal, group % 2))
    rounds = [None] * len(edges)
    for first in range(len(edges)):
        if rounds[first] is not None:
            continue
        edge, colour, by_source = first, 0, True
        while edge is not None and rounds[edge] is None:
            rounds[edge] = colour
            side = 0 if by_source else 1
            following = [
                e
                for e in range(len(edges))
                if e != edge and edges[e][side] == edges[edge][side] and rounds[e] is None
            ]
            edge = following[0] if following else None
            colour, by_source = 1 - colour, not by_source
    tables, moves = [], []
    for colour in range(2):
        table = np.zeros((2, 8), np.int32)
        pairs = []
        for edge, (source, goal, local) in enumerate(edges):
            if rounds[edge] == colour:
                table[source] = local
                pairs.append((source[0] * 8 + source[1], goal[0] * 8 + goal[1]))
        assert len({a for a, _ in pairs}) == 16 and len({b for _, b in pairs}) == 16
        tables.append(table)
        moves.append(sorted(pairs))
    return tables, moves


def shift(step):
    return [(i, (i + step) % 8) for i in range(8)]


def scatter_sum(parts):
    return [parts[0]] + [lax.ppermute(parts[k], "expert", shift(k)) for k in range(1, 8)]


def ring_gather(mine):
    found = {0: mine}
    up = down = mine
    for k in range(1, 5):
        down = lax.ppermute(down, "expert", shift(-1))
        found[k] = down
        if k < 4:
            up = lax.ppermute(up, "expert", shift(1))
            found[8 - k] = up
    return [found[k] for k in range(8)]


SWAP = [(0, 1), (1, 0)]


def shards(
    residual,
    queries,
    response_key_value,
    prompt_cache,
    lengths,
    out_proj,
    norm_gain,
    gate_up,
    down_proj,
    expert_ids,
    gate_weights,
):
    z = lax.axis_index("expert")
    core = lax.axis_index("core")
    place = z.astype(jnp.int32).reshape(1)

    own = prompt_cache.reshape(prompt_cache.shape[1], 2 * HEAD)
    near = lax.ppermute(own, "core", SWAP)
    far = lax.ppermute(own, "xh", SWAP)
    far_near = lax.ppermute(far, "core", SWAP)

    tables, moves = weight_plan()
    ups, downs = [], []
    for table, pairs in zip(tables, moves):
        local = jnp.asarray(table)[core, z]
        up = lax.dynamic_index_in_dim(gate_up, local, 0, keepdims=False)
        down = lax.dynamic_index_in_dim(down_proj, local, 0, keepdims=False)
        ups.append(lax.ppermute(up, ("core", "expert"), pairs))
        downs.append(lax.ppermute(down, ("core", "expert"), pairs))

    turn = z * CHUNK
    ids = lax.dynamic_slice_in_dim(jnp.concatenate([expert_ids] * 2), turn, ROWS, 0)
    weights = lax.dynamic_slice_in_dim(jnp.concatenate([gate_weights] * 2), turn, ROWS, 0)
    send, mix = routing(place, ids, weights)

    response = response_key_value.reshape(ROWS, 2 * HEAD)
    partial = attention(
        place, lengths, queries, response, own, near, far, far_near, out_proj
    )
    hidden, normed = norm(place, residual, norm_gain.reshape(1, WIDTH), scatter_sum(partial))
    outgoing = dispatch(send, ring_gather(normed))
    mine = lax.all_to_all(outgoing, ("prompt", "xh"), split_axis=0, concat_axis=0, tiled=True)
    other = lax.ppermute(mine, "core", SWAP)
    done_mine = experts(mine, ups, downs, F32)
    done_other = experts(other, ups, downs, BF16)
    done = (done_mine + lax.ppermute(done_other, "core", SWAP).astype(F32)).astype(BF16)
    back = lax.all_to_all(done, ("prompt", "xh"), split_axis=0, concat_axis=0, tiled=True)
    return finish(hidden, scatter_sum(combine(mix, back)))


def solution(mesh):
    fine = Mesh(mesh.devices.reshape(8, 2, 2, 8), ("prompt", "xh", "core", "expert"))
    sample = ("prompt", "xh", "core")
    placed = (
        P(sample, None),
        P(sample, "expert"),
        P(sample, "expert", None),
        P("prompt", ("xh", "core"), "expert", None),
        P(sample),
        P("expert", None),
        P(),
        P(sample, None, "expert"),
        P(sample, "expert", None),
        P(sample, None),
        P(sample, None),
    )
    return jax.shard_map(
        shards,
        mesh=fine,
        in_specs=placed,
        out_specs=P((*sample, "expert"), None),
        check_vma=False,
    )
```

```python
import functools
import math

import jax
import jax.numpy as jnp
from jax import lax
from jax.experimental import pallas as pl
from jax.experimental.pallas import tpu as pltpu
from jax.sharding import Mesh, PartitionSpec as P

F32 = jnp.float32
BF16 = jnp.bfloat16
ROWS = 256
CHUNK = 32
WIDTH = 2880
WIDE = 2944
HEAD = 64
CAP = 20
PAD_CAP = 24
CHIPS = 16
SLOTS = CHIPS * PAD_CAP
KEY_BLOCK = 1024
UP_ROWS = 368
UNITS = 192
VMEM_LIMIT = 48 * 1024 * 1024
COLUMN_CUTS = ((0, 768), (768, 1536), (1536, 2304), (2304, 2880))


def params(count=0):
    if count:
        return pltpu.CompilerParams(
            vmem_limit_bytes=VMEM_LIMIT, dimension_semantics=("arbitrary",) * count
        )
    return pltpu.CompilerParams(vmem_limit_bytes=VMEM_LIMIT)


def whole(shape):
    return pl.BlockSpec(shape, lambda *_: (0,) * len(shape))


def spread_cache(kv, keys_ref, even_ref, odd_ref, start):
    rows = kv.shape[0]
    wide = kv.astype(F32)
    turned = pltpu.roll(wide, HEAD, 1)
    first = lax.broadcasted_iota(jnp.int32, wide.shape, 1) < HEAD
    keys_ref[pl.ds(start, rows), :] = jnp.where(first, wide, turned).astype(BF16)
    even_ref[pl.ds(start, rows), :] = jnp.where(first, turned, 1.0).astype(BF16)
    odd_ref[pl.ds(start, rows), :] = jnp.where(first, 1.0, wide).astype(BF16)


def spread_queries(block):
    scaled = block.astype(F32) * (HEAD ** -0.5 * math.log2(math.e))
    high = scaled.astype(BF16).astype(F32)
    low = scaled - high
    first = lax.broadcasted_iota(jnp.int32, scaled.shape, 1) < HEAD
    even = jnp.where(first, high, pltpu.roll(low, HEAD, 1)).astype(BF16)
    odd = jnp.where(first, pltpu.roll(high, HEAD, 1), low).astype(BF16)
    return even, odd


def scores_of(queries, keys):
    return lax.dot_general(
        queries, keys, (((1,), (1,)), ((), ())), preferred_element_type=F32
    )


def attend(pair, keys_ref, values, cuts, states, allowed):
    items = [(side, start, size) for side in range(2) for start, size in cuts]

    def scores(side, start, size):
        found = scores_of(pair[side], keys_ref[start : start + size, :])
        if allowed is not None and start == 0:
            found = jnp.where(allowed, found, -1e30)
        return found

    ahead = scores(*items[0])
    for n, (side, start, size) in enumerate(items):
        here, ahead = ahead, scores(*items[n + 1]) if n + 1 < len(items) else None
        top, total = states[side]
        new_top = jnp.max(here, axis=1, keepdims=True)
        if top is not None:
            new_top = jnp.maximum(top, new_top)
        raised = jnp.exp2(here - new_top).astype(BF16)
        part = jnp.dot(
            raised, values[side][start : start + size, :], preferred_element_type=F32
        )
        if top is not None:
            part = part + total * jnp.exp2(top - new_top)
        states[side] = (new_top, part)
    return states


def first_kernel(
    length_ref, q_ref, resp_ref, own_ref, near_ref, top_ref, total_ref, keys, even, odd
):
    piece = own_ref.shape[0]

    @pl.when(pl.program_id(0) == 0)
    def _():
        spread_cache(resp_ref[...], keys, even, odd, 0)
        spread_cache(own_ref[...], keys, even, odd, ROWS)
        spread_cache(near_ref[...], keys, even, odd, ROWS + piece)

    row = lax.broadcasted_iota(jnp.int32, (ROWS, ROWS), 0)
    col = lax.broadcasted_iota(jnp.int32, (ROWS, ROWS), 1)
    allowed = (col <= row) & (col < length_ref[0])
    cuts = [(0, ROWS)] + [
        (ROWS + start, KEY_BLOCK) for start in range(0, 2 * piece, KEY_BLOCK)
    ]
    pair = spread_queries(q_ref[...])
    states = attend(pair, keys, (even, odd), cuts, [(None, None)] * 2, allowed)
    for side, (top, total) in enumerate(states):
        top_ref[side] = jnp.broadcast_to(top, (ROWS, 2 * HEAD))
        total_ref[side] = total


def second_kernel(
    place_ref, q_ref, a_ref, b_ref, top_ref, total_ref, proj_ref, *rest
):
    outs, (keys, even, odd, attended, turned) = rest[:8], rest[8:]
    piece = a_ref.shape[0]
    step = pl.program_id(0)

    @pl.when(step == 0)
    def _():
        spread_cache(a_ref[...], keys, even, odd, 0)
        spread_cache(b_ref[...], keys, even, odd, piece)

    cuts = [(start, KEY_BLOCK) for start in range(0, 2 * piece, KEY_BLOCK)]
    pair = spread_queries(q_ref[...])
    states = [(top_ref[side][:, :1], total_ref[side]) for side in range(2)]
    states = attend(pair, keys, (even, odd), cuts, states, None)
    totals = [total for _, total in states]
    first = lax.broadcasted_iota(jnp.int32, (ROWS, 2 * HEAD), 1) < HEAD
    numerator = jnp.where(first, totals[0], totals[1])
    denominator = jnp.where(
        first, pltpu.roll(totals[0], HEAD, 1), pltpu.roll(totals[1], HEAD, 1)
    )
    attended[step] = (numerator / denominator).astype(BF16)

    @pl.when(step == pl.num_programs(0) - 1)
    def _():
        for k in range(8):
            source = pl.multiple_of(lax.rem(place_ref[0] + k, 8) * CHUNK, CHUNK)
            for j in range(4):
                turned[CHUNK * k : CHUNK * (k + 1), 128 * j : 128 * (j + 1)] = attended[
                    j, pl.ds(source, CHUNK), :
                ]
        rows = turned[...]
        for low, high in COLUMN_CUTS:
            part = scores_of(rows, proj_ref[low:high, :]).astype(BF16)
            for k in range(8):
                outs[k][:, low:high] = part[CHUNK * k : CHUNK * (k + 1)]


QUERY_SPEC = pl.BlockSpec((ROWS, 2 * HEAD), lambda i: (0, i))
STATE_SPEC = pl.BlockSpec((2, ROWS, 2 * HEAD), lambda i: (i, 0, 0))


def spread_scratch(rows):
    return [pltpu.VMEM((rows, 2 * HEAD), BF16)] * 3


def attend_cost(piece):
    return pl.CostEstimate(
        flops=8 * ROWS * 4 * 2 * HEAD * 2 * piece,
        bytes_accessed=5 << 20,
        transcendentals=8 * ROWS * 2 * piece,
    )


def attend_near(lengths, queries, response, own, near):
    pairs = queries.shape[1] // (2 * HEAD)
    piece = own.shape[0]
    state = (2 * pairs, ROWS, 2 * HEAD)
    return pl.pallas_call(
        first_kernel,
        grid=(pairs,),
        in_specs=[
            pl.BlockSpec(memory_space=pltpu.SMEM),
            QUERY_SPEC,
            whole((ROWS, 2 * HEAD)),
            whole((piece, 2 * HEAD)),
            whole((piece, 2 * HEAD)),
        ],
        out_specs=[STATE_SPEC] * 2,
        out_shape=[jax.ShapeDtypeStruct(state, F32)] * 2,
        scratch_shapes=spread_scratch(ROWS + 2 * piece),
        compiler_params=params(1),
        cost_estimate=attend_cost(piece),
        name="attend_near",
    )(lengths, queries, response, own, near)


def attend_far(place, queries, far, far_near, top, total, out_proj):
    pairs = queries.shape[1] // (2 * HEAD)
    piece = far.shape[0]
    return pl.pallas_call(
        second_kernel,
        grid=(pairs,),
        in_specs=[
            pl.BlockSpec(memory_space=pltpu.SMEM),
            QUERY_SPEC,
            whole((piece, 2 * HEAD)),
            whole((piece, 2 * HEAD)),
            STATE_SPEC,
            STATE_SPEC,
            whole(out_proj.shape),
        ],
        out_specs=[whole((CHUNK, WIDTH))] * 8,
        out_shape=[jax.ShapeDtypeStruct((CHUNK, WIDTH), BF16)] * 8,
        scratch_shapes=spread_scratch(2 * piece)
        + [pltpu.VMEM((pairs, ROWS, 2 * HEAD), BF16), pltpu.VMEM((ROWS, queries.shape[1]), BF16)],
        compiler_params=params(1),
        cost_estimate=attend_cost(piece),
        name="attend_far",
    )(place, queries, far, far_near, top, total, out_proj)


def routing_kernel(place_ref, ids_ref, weights_ref, send_ref, mix_ref):
    ids = ids_ref[...]
    weights = weights_ref[...]
    routes = ids.shape[1]
    expert = lax.broadcasted_iota(jnp.int32, (ROWS, 128), 1)
    named = [ids[:, r : r + 1] == expert for r in range(routes)]
    count = sum(jnp.where(n, 1.0, 0.0) for n in named)
    row = lax.broadcasted_iota(jnp.int32, (ROWS, ROWS), 0)
    col = lax.broadcasted_iota(jnp.int32, (ROWS, ROWS), 1)
    earlier = jnp.dot(
        jnp.where(col < row, 1.0, 0.0).astype(BF16),
        count.astype(BF16),
        preferred_element_type=F32,
    )
    slot = lax.broadcasted_iota(jnp.int32, (ROWS, SLOTS), 1)
    group = lax.rem(place_ref[0], 4)
    send = jnp.zeros((ROWS, SLOTS), F32)
    mix = jnp.zeros((ROWS, SLOTS), F32)
    for r in range(routes):
        rank = jnp.sum(jnp.where(named[r], earlier, 0.0), axis=1, keepdims=True)
        chosen = ids[:, r : r + 1]
        chip = lax.shift_right_logical(chosen, 2)
        mine = lax.bitwise_and(chosen, 3) == group
        at = jnp.where(mine, chip * PAD_CAP + rank.astype(jnp.int32), -1)
        hit = slot == at
        send = send + jnp.where(hit, 1.0, 0.0)
        mix = mix + jnp.where(hit, weights[:, r : r + 1], 0.0)
    send_ref[...] = jnp.transpose(send).astype(BF16)
    high = mix.astype(BF16)
    mix_ref[:, :SLOTS] = high
    mix_ref[:, SLOTS:] = (mix - high.astype(F32)).astype(BF16)


def routing(place, ids, weights):
    return pl.pallas_call(
        routing_kernel,
        in_specs=[
            pl.BlockSpec(memory_space=pltpu.SMEM),
            whole(ids.shape),
            whole(weights.shape),
        ],
        grid=(1,),
        out_specs=[whole((SLOTS, ROWS)), whole((ROWS, 2 * SLOTS))],
        out_shape=[
            jax.ShapeDtypeStruct((SLOTS, ROWS), BF16),
            jax.ShapeDtypeStruct((ROWS, 2 * SLOTS), BF16),
        ],
        compiler_params=params(1),
        name="routing",
    )(place, ids, weights)


def norm_kernel(place_ref, residual_ref, gain_ref, *refs):
    parts, (hidden_ref, normed_ref) = refs[:3], refs[3:]
    projected = parts[0][...].astype(F32)
    for part in parts[1:]:
        projected = projected + part[...].astype(F32)
    hidden = residual_ref[...].astype(F32) + projected
    inverse = lax.rsqrt(jnp.mean(hidden * hidden, axis=1, keepdims=True) + 1e-5)
    hidden_ref[...] = hidden
    normed_ref[...] = (hidden * inverse * gain_ref[...]).astype(BF16)


def norm(place, residual, gain, parts):
    chunk = (CHUNK, WIDTH)
    return pl.pallas_call(
        norm_kernel,
        grid_spec=pltpu.PrefetchScalarGridSpec(
            num_scalar_prefetch=1,
            grid=(1,),
            in_specs=[
                pl.BlockSpec(chunk, lambda i, place: (place[0], 0)),
                pl.BlockSpec((1, WIDTH), lambda i, place: (0, 0)),
            ]
            + [pl.BlockSpec(chunk, lambda i, place: (0, 0))] * 3,
            out_specs=[pl.BlockSpec(chunk, lambda i, place: (0, 0))] * 2,
        ),
        out_shape=[jax.ShapeDtypeStruct(chunk, F32), jax.ShapeDtypeStruct(chunk, BF16)],
        compiler_params=params(1),
        name="norm",
    )(place, residual, gain, *parts)


def dispatch_kernel(send_ref, *refs):
    parts, (out_ref, rows) = refs[:8], refs[8:]
    for k in range(8):
        rows[CHUNK * k : CHUNK * (k + 1), :] = parts[k][...]
    for low, high in COLUMN_CUTS:
        out_ref[:, low:high] = jnp.dot(
            send_ref[...], rows[:, low:high], preferred_element_type=F32
        ).astype(BF16)


def dispatch(send, parts):
    return pl.pallas_call(
        dispatch_kernel,
        grid=(1,),
        in_specs=[whole(send.shape)] + [whole((CHUNK, WIDTH))] * 8,
        out_specs=whole((SLOTS, WIDE)),
        out_shape=jax.ShapeDtypeStruct((SLOTS, WIDE), BF16),
        scratch_shapes=[pltpu.VMEM((ROWS, WIDTH), BF16)],
        compiler_params=params(1),
        name="dispatch",
    )(send, *parts)


def combine_kernel(mix_ref, back_ref, *outs):
    for low, high in COLUMN_CUTS:
        block = back_ref[:, low:high]
        part = jnp.dot(mix_ref[:, :SLOTS], block, preferred_element_type=F32)
        part = part + jnp.dot(mix_ref[:, SLOTS:], block, preferred_element_type=F32)
        part = part.astype(BF16)
        for k in range(8):
            outs[k][:, low:high] = part[CHUNK * k : CHUNK * (k + 1)]


def combine(mix, back):
    return pl.pallas_call(
        combine_kernel,
        grid=(1,),
        in_specs=[whole(mix.shape), whole(back.shape)],
        out_specs=[whole((CHUNK, WIDTH))] * 8,
        out_shape=[jax.ShapeDtypeStruct((CHUNK, WIDTH), BF16)] * 8,
        compiler_params=params(1),
        name="combine",
    )(mix, back)


def finish_kernel(hidden_ref, *refs):
    parts, out_ref = refs[:3], refs[3]
    total = parts[0][...].astype(F32)
    for part in parts[1:]:
        total = total + part[...].astype(F32)
    out_ref[...] = (hidden_ref[...] + total).astype(BF16)


def finish(hidden, parts):
    return pl.pallas_call(
        finish_kernel,
        grid=(1,),
        in_specs=[whole((CHUNK, WIDTH))] * 4,
        out_specs=whole((CHUNK, WIDTH)),
        out_shape=jax.ShapeDtypeStruct((CHUNK, WIDTH), BF16),
        compiler_params=params(1),
        name="finish",
    )(hidden, *parts)


def pack_kernel(_, up_ref, down_ref, out_ref):
    double, units = up_ref.shape[1], down_ref.shape[0]
    pad = jnp.zeros((UP_ROWS - double, WIDTH), BF16)
    out_ref[:UP_ROWS, :] = jnp.concatenate([up_ref[0], pad])
    pad = jnp.zeros((UNITS - units, WIDTH), BF16)
    out_ref[UP_ROWS:, :] = jnp.concatenate([down_ref[...], pad])


def pack(local, ups, down):
    shape = (UP_ROWS + UNITS, WIDTH)
    return pl.pallas_call(
        pack_kernel,
        grid_spec=pltpu.PrefetchScalarGridSpec(
            num_scalar_prefetch=1,
            grid=(1,),
            in_specs=[
                pl.BlockSpec((1, *ups.shape[1:]), lambda i, local: (local[0], 0, 0)),
                pl.BlockSpec(down.shape, lambda i, local: (0, 0)),
            ],
            out_specs=pl.BlockSpec(shape, lambda i, local: (0, 0)),
        ),
        out_shape=jax.ShapeDtypeStruct(shape, BF16),
        compiler_params=params(1),
        name="pack",
    )(local, ups, down)


def activation(x, rows, units):
    shape = (rows.shape[0], units)
    row = lax.broadcasted_iota(jnp.int32, shape, 0)
    col = lax.broadcasted_iota(jnp.int32, shape, 1)
    pick = jnp.where(row == 2 * col, 1.0, 0.0).astype(BF16)
    both = scores_of(x, rows)
    up = jnp.concatenate([both[:, 1:], both[:, :1]], axis=1)
    act = ((up + 1.0) * both * jax.nn.sigmoid(1.702 * both)).astype(BF16)
    return jnp.dot(act, pick, preferred_element_type=F32).astype(BF16)


def open_kernel(x_ref, up_ref, out_ref):
    out_ref[...] = activation(x_ref[:, :WIDTH], up_ref[...], out_ref.shape[1])


def close_kernel(x_ref, act_ref, down_ref, piece_ref, out_ref):
    acts = act_ref[...], activation(x_ref[:, :WIDTH], piece_ref[:UP_ROWS, :], UNITS)
    for low, high in COLUMN_CUTS:
        total = jnp.dot(acts[0], down_ref[:, low:high], preferred_element_type=F32)
        total = total + jnp.dot(
            acts[1], piece_ref[UP_ROWS:, low:high], preferred_element_type=F32
        )
        out_ref[:, low:high] = total.astype(out_ref.dtype)


def expert_cost(rows, flops):
    return pl.CostEstimate(
        flops=rows * flops, bytes_accessed=6 << 20, transcendentals=rows * 360
    )


def open_experts(x, up):
    shape = (x.shape[0], up.shape[0] // 2)
    return pl.pallas_call(
        open_kernel,
        grid=(1,),
        in_specs=[whole(x.shape), whole(up.shape)],
        out_specs=whole(shape),
        out_shape=jax.ShapeDtypeStruct(shape, BF16),
        compiler_params=params(1),
        cost_estimate=expert_cost(shape[0], WIDTH * 720),
        name="open_experts",
    )(x, up)


def close_experts(x, act, down, piece):
    rows = x.shape[0]
    return pl.pallas_call(
        close_kernel,
        grid=(1,),
        in_specs=[whole(w.shape) for w in (x, act, down, piece)],
        out_specs=whole((rows, WIDE)),
        out_shape=jax.ShapeDtypeStruct((rows, WIDE), BF16),
        compiler_params=params(1),
        cost_estimate=expert_cost(rows, WIDTH * 1440),
        name="close_experts",
    )(x, act, down, piece)


MOVES = (
    ((1, 0), (7, 8), (0, 1), (2, 9), (9, 10), (12, 2), (11, 11), (10, 3))
    + ((3, 4), (5, 12), (6, 5), (4, 13), (14, 14), (8, 6), (13, 15), (15, 7)),
    ((0, 0), (2, 8), (7, 1), (1, 9), (10, 10), (11, 2), (12, 11), (9, 3))
    + ((6, 4), (4, 12), (3, 5), (5, 13), (15, 14), (13, 6), (14, 15), (8, 7)),
)
SENT = tuple(sum((goal % 2) << source for source, goal in moves) for moves in MOVES)


def shift(step):
    return [(i, (i + step) % 8) for i in range(8)]


def tie(*values):
    return lax.optimization_barrier(values)


def add(a, b):
    return (a.astype(F32) + b.astype(F32)).astype(BF16)


def ring_sum(parts):
    down, up = parts[4], parts[3]
    for k in (5, 6, 7):
        down = add(lax.ppermute(down, "expert", shift(-1)), parts[k])
        up = lax.ppermute(up, "expert", shift(1))
        if k < 7:
            up = add(up, parts[7 - k])
    return [parts[0], up, lax.ppermute(down, "expert", shift(-1))]


def ring_gather(mine, beside):
    found = {0: mine}
    up = down = mine
    for k in range(1, 5):
        if k == 4:
            *beside, down = tie(*beside, down)
        down = lax.ppermute(down, "expert", shift(-1))
        found[k] = down
        if k < 4:
            up = lax.ppermute(up, "expert", shift(1))
            found[8 - k] = up
    return beside, [found[k] for k in range(8)]


SWAP = [(0, 1), (1, 0)]


def shards(
    residual,
    queries,
    response_key_value,
    prompt_cache,
    lengths,
    out_proj,
    norm_gain,
    gate_up,
    down_proj,
    expert_ids,
    gate_weights,
):
    z = lax.axis_index("expert")
    core = lax.axis_index("core")
    place = z.astype(jnp.int32).reshape(1)

    own = prompt_cache.reshape(prompt_cache.shape[1], 2 * HEAD)
    near = lax.ppermute(own, "core", SWAP)
    far = lax.ppermute(own, "xh", SWAP)

    gate_up = jnp.transpose(gate_up, (0, 2, 1))
    device = core * 8 + z
    chosen = [
        lax.bitwise_and(lax.shift_right_logical(jnp.int32(table), device), 1) for table in SENT
    ]

    def send_weights(piece, n):
        return lax.ppermute(piece, ("core", "expert"), MOVES[n])

    def pick(array, n):
        return lax.dynamic_index_in_dim(array, chosen[n], 0, keepdims=False)

    up, near = tie(pick(gate_up, 0), near)
    up_first = send_weights(up, 0)
    response = response_key_value.reshape(ROWS, 2 * HEAD)
    top, total = attend_near(lengths, queries, response, own, near)

    down, far, top = tie(pick(down_proj, 0), far, top)
    down_first = send_weights(down, 0)
    far_near = lax.ppermute(far, "core", SWAP)
    partial = attend_far(place, queries, far, far_near, top, total, out_proj.T)
    up_first, down_first, *partial = tie(up_first, down_first, *partial)

    turn, partial[0] = tie(z * CHUNK, partial[0])
    ids = lax.dynamic_slice_in_dim(jnp.concatenate([expert_ids] * 2), turn, ROWS, 0)
    weights = lax.dynamic_slice_in_dim(jnp.concatenate([gate_weights] * 2), turn, ROWS, 0)
    send, mix = routing(place, ids, weights)
    hidden, normed = norm(place, residual, norm_gain.reshape(1, WIDTH), ring_sum(partial))

    gate_up, down_proj, normed = tie(gate_up, down_proj, normed)
    piece = pack(chosen[1].reshape(1), gate_up, pick(down_proj, 1))
    (piece, send, mix), gathered = ring_gather(normed, (piece, send, mix))
    outgoing = dispatch(send, gathered)
    second = send_weights(piece, 1)
    mine = lax.all_to_all(outgoing, ("prompt", "xh"), split_axis=0, concat_axis=0, tiled=True)
    other = lax.ppermute(mine, "core", SWAP)
    act_mine = open_experts(mine, up_first)
    act_other = open_experts(other, up_first)
    second, act_mine, act_other = tie(second, act_mine, act_other)
    done_other = close_experts(other, act_other, down_first, second)
    done_mine = close_experts(mine, act_mine, down_first, second)
    done = add(done_mine, lax.ppermute(done_other, "core", SWAP))
    back = lax.all_to_all(done, ("prompt", "xh"), split_axis=0, concat_axis=0, tiled=True)
    return finish(hidden, ring_sum(combine(mix, back)))


def solution(mesh):
    fine = Mesh(mesh.devices.reshape(8, 2, 2, 8), ("prompt", "xh", "core", "expert"))
    sample = ("prompt", "xh", "core")
    placed = (
        P(sample, None),
        P(sample, "expert"),
        P(sample, "expert", None),
        P("prompt", ("xh", "core"), "expert", None),
        P(sample),
        P("expert", None),
        P(),
        P(sample, None, "expert"),
        P(sample, "expert", None),
        P(sample, None),
        P(sample, None),
    )
    return jax.shard_map(
        shards,
        mesh=fine,
        in_specs=placed,
        out_specs=P((*sample, "expert"), None),
        check_vma=False,
    )
```

```python
import functools
import math

import jax
import jax.numpy as jnp
from jax import lax
from jax.experimental import pallas as pl
from jax.experimental.pallas import tpu as pltpu
from jax.sharding import Mesh, PartitionSpec as P

F32 = jnp.float32
BF16 = jnp.bfloat16
ROWS = 256
CHUNK = 32
PIECES = (0, 32, 64, 96, 128, 144, 160, 192, 224, 256)
WIDTH = 2880
WIDE = 2944
HEAD = 64
CAP = 20
PAD_CAP = 24
CHIPS = 16
SLOTS = CHIPS * PAD_CAP
KEY_BLOCK = 1024
UP_ROWS = 368
UNITS = 192
VMEM_LIMIT = 24 * 1024 * 1024
COLUMN_CUTS = ((0, 768), (768, 1536), (1536, 2304), (2304, 2880))


def params(count=0):
    if count:
        return pltpu.CompilerParams(
            vmem_limit_bytes=VMEM_LIMIT, dimension_semantics=("arbitrary",) * count
        )
    return pltpu.CompilerParams(vmem_limit_bytes=VMEM_LIMIT)


def spill(part, outs, low, high):
    part = part.astype(BF16)
    for out, start, stop in zip(outs, PIECES, PIECES[1:]):
        out[:, low:high] = part[start:stop]


PIECE_SHAPES = [(stop - start, WIDTH) for start, stop in zip(PIECES, PIECES[1:])]


def whole(shape):
    return pl.BlockSpec(shape, lambda *_: (0,) * len(shape))


def spread_cache(kv, keys_ref, even_ref, odd_ref, start):
    rows = kv.shape[0]
    wide = kv.astype(F32)
    turned = pltpu.roll(wide, HEAD, 1)
    first = lax.broadcasted_iota(jnp.int32, wide.shape, 1) < HEAD
    keys_ref[pl.ds(start, rows), :] = jnp.where(first, wide, turned).astype(BF16)
    even_ref[pl.ds(start, rows), :] = jnp.where(first, turned, 1.0).astype(BF16)
    odd_ref[pl.ds(start, rows), :] = jnp.where(first, 1.0, wide).astype(BF16)


def spread_queries(block):
    scaled = block.astype(F32) * (HEAD ** -0.5 * math.log2(math.e))
    high = scaled.astype(BF16).astype(F32)
    low = scaled - high
    first = lax.broadcasted_iota(jnp.int32, scaled.shape, 1) < HEAD
    even = jnp.where(first, high, pltpu.roll(low, HEAD, 1)).astype(BF16)
    odd = jnp.where(first, pltpu.roll(high, HEAD, 1), low).astype(BF16)
    return even, odd


def scores_of(queries, keys):
    return lax.dot_general(
        queries, keys, (((1,), (1,)), ((), ())), preferred_element_type=F32
    )


def attend(pair, keys_ref, values, cuts, states, allowed):
    items = [(side, start, size) for side in range(2) for start, size in cuts]

    def scores(side, start, size):
        found = scores_of(pair[side], keys_ref[start : start + size, :])
        if allowed is not None and start == 0:
            found = jnp.where(allowed, found, -1e30)
        return found

    ahead = scores(*items[0])
    for n, (side, start, size) in enumerate(items):
        here, ahead = ahead, scores(*items[n + 1]) if n + 1 < len(items) else None
        top, total = states[side]
        new_top = jnp.max(here, axis=1, keepdims=True)
        if top is not None:
            new_top = jnp.maximum(top, new_top)
        raised = jnp.exp2(here - new_top).astype(BF16)
        part = jnp.dot(
            raised, values[side][start : start + size, :], preferred_element_type=F32
        )
        if top is not None:
            part = part + total * jnp.exp2(top - new_top)
        states[side] = (new_top, part)
    return states


def first_kernel(
    length_ref, q_ref, resp_ref, own_ref, near_ref, top_ref, total_ref, keys, even, odd
):
    piece = own_ref.shape[0]

    @pl.when(pl.program_id(0) == 0)
    def _():
        spread_cache(resp_ref[...], keys, even, odd, 0)
        spread_cache(own_ref[...], keys, even, odd, ROWS)
        spread_cache(near_ref[...], keys, even, odd, ROWS + piece)

    row = lax.broadcasted_iota(jnp.int32, (ROWS, ROWS), 0)
    col = lax.broadcasted_iota(jnp.int32, (ROWS, ROWS), 1)
    allowed = (col <= row) & (col < length_ref[0])
    cuts = [(0, ROWS)] + [
        (ROWS + start, KEY_BLOCK) for start in range(0, 2 * piece, KEY_BLOCK)
    ]
    pair = spread_queries(q_ref[...])
    states = attend(pair, keys, (even, odd), cuts, [(None, None)] * 2, allowed)
    for side, (top, total) in enumerate(states):
        top_ref[side] = jnp.broadcast_to(top, (ROWS, 2 * HEAD))
        total_ref[side] = total


def second_kernel(
    place_ref, q_ref, a_ref, b_ref, top_ref, total_ref, proj_ref, *rest
):
    outs, (keys, even, odd, attended, turned) = rest[:9], rest[9:]
    piece = a_ref.shape[0]
    step = pl.program_id(0)

    @pl.when(step == 0)
    def _():
        spread_cache(a_ref[...], keys, even, odd, 0)
        spread_cache(b_ref[...], keys, even, odd, piece)

    cuts = [(start, KEY_BLOCK) for start in range(0, 2 * piece, KEY_BLOCK)]
    pair = spread_queries(q_ref[...])
    states = [(top_ref[side][:, :1], total_ref[side]) for side in range(2)]
    states = attend(pair, keys, (even, odd), cuts, states, None)
    totals = [total for _, total in states]
    first = lax.broadcasted_iota(jnp.int32, (ROWS, 2 * HEAD), 1) < HEAD
    numerator = jnp.where(first, totals[0], totals[1])
    denominator = jnp.where(
        first, pltpu.roll(totals[0], HEAD, 1), pltpu.roll(totals[1], HEAD, 1)
    )
    attended[step] = (numerator / denominator).astype(BF16)

    @pl.when(step == pl.num_programs(0) - 1)
    def _():
        for k in range(8):
            source = pl.multiple_of(lax.rem(place_ref[0] + k, 8) * CHUNK, CHUNK)
            for j in range(4):
                turned[CHUNK * k : CHUNK * (k + 1), 128 * j : 128 * (j + 1)] = attended[
                    j, pl.ds(source, CHUNK), :
                ]
        rows = turned[...]
        for low, high in COLUMN_CUTS:
            spill(scores_of(rows, proj_ref[low:high, :]), outs, low, high)


QUERY_SPEC = pl.BlockSpec((ROWS, 2 * HEAD), lambda i: (0, i))
STATE_SPEC = pl.BlockSpec((2, ROWS, 2 * HEAD), lambda i: (i, 0, 0))


def spread_scratch(rows):
    return [pltpu.VMEM((rows, 2 * HEAD), BF16)] * 3


def attend_cost(piece):
    return pl.CostEstimate(
        flops=8 * ROWS * 4 * 2 * HEAD * 2 * piece,
        bytes_accessed=5 << 20,
        transcendentals=8 * ROWS * 2 * piece,
    )


def attend_near(lengths, queries, response, own, near):
    pairs = queries.shape[1] // (2 * HEAD)
    piece = own.shape[0]
    state = (2 * pairs, ROWS, 2 * HEAD)
    return pl.pallas_call(
        first_kernel,
        grid=(pairs,),
        in_specs=[
            pl.BlockSpec(memory_space=pltpu.SMEM),
            QUERY_SPEC,
            whole((ROWS, 2 * HEAD)),
            whole((piece, 2 * HEAD)),
            whole((piece, 2 * HEAD)),
        ],
        out_specs=[STATE_SPEC] * 2,
        out_shape=[jax.ShapeDtypeStruct(state, F32)] * 2,
        scratch_shapes=spread_scratch(ROWS + 2 * piece),
        compiler_params=params(1),
        cost_estimate=attend_cost(piece),
        name="attend_near",
    )(lengths, queries, response, own, near)


def attend_far(place, queries, far, far_near, top, total, out_proj):
    pairs = queries.shape[1] // (2 * HEAD)
    piece = far.shape[0]
    return pl.pallas_call(
        second_kernel,
        grid=(pairs,),
        in_specs=[
            pl.BlockSpec(memory_space=pltpu.SMEM),
            QUERY_SPEC,
            whole((piece, 2 * HEAD)),
            whole((piece, 2 * HEAD)),
            STATE_SPEC,
            STATE_SPEC,
            whole(out_proj.shape),
        ],
        out_specs=[whole(shape) for shape in PIECE_SHAPES],
        out_shape=[jax.ShapeDtypeStruct(shape, BF16) for shape in PIECE_SHAPES],
        scratch_shapes=spread_scratch(2 * piece)
        + [pltpu.VMEM((pairs, ROWS, 2 * HEAD), BF16), pltpu.VMEM((ROWS, queries.shape[1]), BF16)],
        compiler_params=params(1),
        cost_estimate=attend_cost(piece),
        name="attend_far",
    )(place, queries, far, far_near, top, total, out_proj)


def routing_kernel(place_ref, ids_ref, weights_ref, send_ref, mix_ref):
    ids = ids_ref[...]
    weights = weights_ref[...]
    routes = ids.shape[1]
    expert = lax.broadcasted_iota(jnp.int32, (ROWS, 128), 1)
    named = [ids[:, r : r + 1] == expert for r in range(routes)]
    count = sum(jnp.where(n, 1.0, 0.0) for n in named)
    row = lax.broadcasted_iota(jnp.int32, (ROWS, ROWS), 0)
    col = lax.broadcasted_iota(jnp.int32, (ROWS, ROWS), 1)
    earlier = jnp.dot(
        jnp.where(col < row, 1.0, 0.0).astype(BF16),
        count.astype(BF16),
        preferred_element_type=F32,
    )
    slot = lax.broadcasted_iota(jnp.int32, (ROWS, SLOTS), 1)
    group = lax.rem(place_ref[0], 4)
    send = jnp.zeros((ROWS, SLOTS), F32)
    mix = jnp.zeros((ROWS, SLOTS), F32)
    for r in range(routes):
        rank = jnp.sum(jnp.where(named[r], earlier, 0.0), axis=1, keepdims=True)
        chosen = ids[:, r : r + 1]
        chip = lax.shift_right_logical(chosen, 2)
        mine = lax.bitwise_and(chosen, 3) == group
        at = jnp.where(mine, chip * PAD_CAP + rank.astype(jnp.int32), -1)
        hit = slot == at
        send = send + jnp.where(hit, 1.0, 0.0)
        mix = mix + jnp.where(hit, weights[:, r : r + 1], 0.0)
    send_ref[...] = jnp.transpose(send).astype(BF16)
    high = mix.astype(BF16)
    mix_ref[:, :SLOTS] = high
    mix_ref[:, SLOTS:] = (mix - high.astype(F32)).astype(BF16)


def routing(place, ids, weights):
    return pl.pallas_call(
        routing_kernel,
        in_specs=[
            pl.BlockSpec(memory_space=pltpu.SMEM),
            whole(ids.shape),
            whole(weights.shape),
        ],
        grid=(1,),
        out_specs=[whole((SLOTS, ROWS)), whole((ROWS, 2 * SLOTS))],
        out_shape=[
            jax.ShapeDtypeStruct((SLOTS, ROWS), BF16),
            jax.ShapeDtypeStruct((ROWS, 2 * SLOTS), BF16),
        ],
        compiler_params=params(1),
        name="routing",
    )(place, ids, weights)


def norm_kernel(place_ref, residual_ref, gain_ref, *refs):
    parts, (hidden_ref, normed_ref) = refs[:5], refs[5:]
    projected = parts[0][...].astype(F32)
    for part in parts[1:]:
        projected = projected + part[...].astype(F32)
    hidden = residual_ref[...].astype(F32) + projected
    inverse = lax.rsqrt(jnp.mean(hidden * hidden, axis=1, keepdims=True) + 1e-5)
    hidden_ref[...] = hidden
    normed_ref[...] = (hidden * inverse * gain_ref[...]).astype(BF16)


def norm(place, residual, gain, parts):
    chunk = (CHUNK, WIDTH)
    return pl.pallas_call(
        norm_kernel,
        grid_spec=pltpu.PrefetchScalarGridSpec(
            num_scalar_prefetch=1,
            grid=(1,),
            in_specs=[
                pl.BlockSpec(chunk, lambda i, place: (place[0], 0)),
                pl.BlockSpec((1, WIDTH), lambda i, place: (0, 0)),
            ]
            + [pl.BlockSpec(chunk, lambda i, place: (0, 0))] * 5,
            out_specs=[pl.BlockSpec(chunk, lambda i, place: (0, 0))] * 2,
        ),
        out_shape=[jax.ShapeDtypeStruct(chunk, F32), jax.ShapeDtypeStruct(chunk, BF16)],
        compiler_params=params(1),
        name="norm",
    )(place, residual, gain, *parts)


def dispatch_kernel(send_ref, *refs):
    parts, (out_ref, rows) = refs[:9], refs[9:]
    for part, start, stop in zip(parts, PIECES, PIECES[1:]):
        rows[start:stop, :] = part[...]
    for low, high in COLUMN_CUTS:
        out_ref[:, low:high] = jnp.dot(
            send_ref[...], rows[:, low:high], preferred_element_type=F32
        ).astype(BF16)


def dispatch(send, parts):
    return pl.pallas_call(
        dispatch_kernel,
        grid=(1,),
        in_specs=[whole(send.shape)] + [whole(shape) for shape in PIECE_SHAPES],
        out_specs=whole((SLOTS, WIDE)),
        out_shape=jax.ShapeDtypeStruct((SLOTS, WIDE), BF16),
        scratch_shapes=[pltpu.VMEM((ROWS, WIDTH), BF16)],
        compiler_params=params(1),
        name="dispatch",
    )(send, *parts)


def combine_kernel(mix_ref, back_ref, *outs):
    for low, high in COLUMN_CUTS:
        block = back_ref[:, low:high]
        part = jnp.dot(mix_ref[:, :SLOTS], block, preferred_element_type=F32)
        part = part + jnp.dot(mix_ref[:, SLOTS:], block, preferred_element_type=F32)
        spill(part, outs, low, high)


def combine(mix, back):
    return pl.pallas_call(
        combine_kernel,
        grid=(1,),
        in_specs=[whole(mix.shape), whole(back.shape)],
        out_specs=[whole(shape) for shape in PIECE_SHAPES],
        out_shape=[jax.ShapeDtypeStruct(shape, BF16) for shape in PIECE_SHAPES],
        compiler_params=params(1),
        name="combine",
    )(mix, back)


def finish_kernel(hidden_ref, *refs):
    parts, out_ref = refs[:5], refs[5]
    total = parts[0][...].astype(F32)
    for part in parts[1:]:
        total = total + part[...].astype(F32)
    out_ref[...] = (hidden_ref[...] + total).astype(BF16)


def finish(hidden, parts):
    return pl.pallas_call(
        finish_kernel,
        grid=(1,),
        in_specs=[whole((CHUNK, WIDTH))] * 6,
        out_specs=whole((CHUNK, WIDTH)),
        out_shape=jax.ShapeDtypeStruct((CHUNK, WIDTH), BF16),
        compiler_params=params(1),
        name="finish",
    )(hidden, *parts)


def pack_kernel(_, up_ref, down_ref, out_ref):
    double, units = up_ref.shape[1], down_ref.shape[0]
    pad = jnp.zeros((UP_ROWS - double, WIDTH), BF16)
    out_ref[:UP_ROWS, :] = jnp.concatenate([up_ref[0], pad])
    pad = jnp.zeros((UNITS - units, WIDTH), BF16)
    out_ref[UP_ROWS:, :] = jnp.concatenate([down_ref[...], pad])


def pack(local, ups, down):
    shape = (UP_ROWS + UNITS, WIDTH)
    return pl.pallas_call(
        pack_kernel,
        grid_spec=pltpu.PrefetchScalarGridSpec(
            num_scalar_prefetch=1,
            grid=(1,),
            in_specs=[
                pl.BlockSpec((1, *ups.shape[1:]), lambda i, local: (local[0], 0, 0)),
                pl.BlockSpec(down.shape, lambda i, local: (0, 0)),
            ],
            out_specs=pl.BlockSpec(shape, lambda i, local: (0, 0)),
        ),
        out_shape=jax.ShapeDtypeStruct(shape, BF16),
        compiler_params=params(1),
        name="pack",
    )(local, ups, down)


def activation(x, rows, units):
    shape = (rows.shape[0], units)
    row = lax.broadcasted_iota(jnp.int32, shape, 0)
    col = lax.broadcasted_iota(jnp.int32, shape, 1)
    pick = jnp.where(row == 2 * col, 1.0, 0.0).astype(BF16)
    both = scores_of(x, rows)
    up = jnp.concatenate([both[:, 1:], both[:, :1]], axis=1)
    act = ((up + 1.0) * both * jax.nn.sigmoid(1.702 * both)).astype(BF16)
    return jnp.dot(act, pick, preferred_element_type=F32).astype(BF16)


def open_kernel(x_ref, up_ref, out_ref):
    out_ref[...] = activation(x_ref[:, :WIDTH], up_ref[...], out_ref.shape[1])


def close_kernel(x_ref, act_ref, down_ref, piece_ref, out_ref):
    acts = act_ref[...], activation(x_ref[:, :WIDTH], piece_ref[:UP_ROWS, :], UNITS)
    for low, high in COLUMN_CUTS:
        total = jnp.dot(acts[0], down_ref[:, low:high], preferred_element_type=F32)
        total = total + jnp.dot(
            acts[1], piece_ref[UP_ROWS:, low:high], preferred_element_type=F32
        )
        out_ref[:, low:high] = total.astype(out_ref.dtype)


def expert_cost(rows, flops):
    return pl.CostEstimate(
        flops=rows * flops, bytes_accessed=6 << 20, transcendentals=rows * 360
    )


def open_experts(x, up):
    shape = (x.shape[0], up.shape[0] // 2)
    return pl.pallas_call(
        open_kernel,
        grid=(1,),
        in_specs=[whole(x.shape), whole(up.shape)],
        out_specs=whole(shape),
        out_shape=jax.ShapeDtypeStruct(shape, BF16),
        compiler_params=params(1),
        cost_estimate=expert_cost(shape[0], WIDTH * 720),
        name="open_experts",
    )(x, up)


def close_experts(x, act, down, piece):
    rows = x.shape[0]
    return pl.pallas_call(
        close_kernel,
        grid=(1,),
        in_specs=[whole(w.shape) for w in (x, act, down, piece)],
        out_specs=whole((rows, WIDE)),
        out_shape=jax.ShapeDtypeStruct((rows, WIDE), BF16),
        compiler_params=params(1),
        cost_estimate=expert_cost(rows, WIDTH * 1440),
        name="close_experts",
    )(x, act, down, piece)


MOVES = (
    ((0, 8), (1, 0), (7, 9), (2, 1), (10, 2), (11, 10), (9, 3), (12, 11))
    + ((5, 12), (3, 4), (6, 13), (4, 5), (8, 6), (13, 14), (15, 7), (14, 15)),
    ((7, 8), (2, 0), (1, 9), (0, 1), (9, 2), (12, 10), (11, 3), (10, 11))
    + ((4, 12), (6, 4), (5, 13), (3, 5), (14, 6), (15, 14), (13, 7), (8, 15)),
)
SENT = tuple(sum((goal % 2) << source for source, goal in moves) for moves in MOVES)


def shift(step):
    return [(i, (i + step) % 8) for i in range(8)]


def tie(*values):
    return lax.optimization_barrier(values)


def add(a, b):
    return (a.astype(F32) + b.astype(F32)).astype(BF16)


def move(chunk, step):
    return lax.ppermute(chunk, "expert", shift(step))


def join_kernel(*refs):
    for side in range(2):
        own, whole_ref, half, out = refs[3 * side : 3 * side + 3] + (refs[6 + side],)
        rows = slice(side * CHUNK // 2, (side + 1) * CHUNK // 2)
        rest = slice((1 - side) * CHUNK // 2, (2 - side) * CHUNK // 2)
        total = own[...].astype(F32) + whole_ref[...].astype(F32)
        out[rest, :] = total[rest].astype(BF16)
        out[rows, :] = (total[rows] + half[...].astype(F32)).astype(BF16)


def join(*parts):
    return pl.pallas_call(
        join_kernel,
        grid=(1,),
        in_specs=[whole(part.shape) for part in parts],
        out_specs=[whole((CHUNK, WIDTH))] * 2,
        out_shape=[jax.ShapeDtypeStruct((CHUNK, WIDTH), BF16)] * 2,
        compiler_params=params(1),
        name="join",
    )(*parts)


def sum_to_owner(parts):
    own, up_1, up_2, up_3, half_down, half_up, down_3, down_2, down_1 = parts
    down, up = join(
        down_2, move(down_3, -1), move(half_down, -2), up_2, move(up_3, 1), move(half_up, 2)
    )
    return [own, move(down_1, -1), move(up_1, 1), move(down, -2), move(up, 2)]


def gather(mine, beside):
    near = move(mine, -1), move(mine, 1)
    *beside, after, before = tie(*beside, move(mine, -2), move(mine, 2))
    half = CHUNK // 2
    far = move(after[:half], -2), move(before[half:], 2)
    third, fifth = move(after, -1), move(before, 1)
    return beside, [mine, near[0], after, third, *far, fifth, before, near[1]]


SWAP = [(0, 1), (1, 0)]


def shards(
    residual,
    queries,
    response_key_value,
    prompt_cache,
    lengths,
    out_proj,
    norm_gain,
    gate_up,
    down_proj,
    expert_ids,
    gate_weights,
):
    z = lax.axis_index("expert")
    core = lax.axis_index("core")
    place = z.astype(jnp.int32).reshape(1)

    own = prompt_cache.reshape(prompt_cache.shape[1], 2 * HEAD)
    near = lax.ppermute(own, "core", SWAP)
    far = lax.ppermute(own, "xh", SWAP)

    gate_up = jnp.transpose(gate_up, (0, 2, 1))
    device = core * 8 + z
    chosen = [
        lax.bitwise_and(lax.shift_right_logical(jnp.int32(table), device), 1) for table in SENT
    ]

    def send_weights(piece, n):
        return lax.ppermute(piece, ("core", "expert"), MOVES[n])

    def pick(array, n):
        return lax.dynamic_index_in_dim(array, chosen[n], 0, keepdims=False)

    up, near = tie(pick(gate_up, 0), near)
    up_first = send_weights(up, 0)
    response = response_key_value.reshape(ROWS, 2 * HEAD)
    top, total = attend_near(lengths, queries, response, own, near)

    down, far, top = tie(pick(down_proj, 0), far, top)
    down_first = send_weights(down, 0)
    far_near = lax.ppermute(far, "core", SWAP)
    partial = attend_far(place, queries, far, far_near, top, total, out_proj.T)
    up_first, down_first, *partial = tie(up_first, down_first, *partial)

    turn, partial[0] = tie(z * CHUNK, partial[0])
    ids = lax.dynamic_slice_in_dim(jnp.concatenate([expert_ids] * 2), turn, ROWS, 0)
    weights = lax.dynamic_slice_in_dim(jnp.concatenate([gate_weights] * 2), turn, ROWS, 0)
    send, mix = routing(place, ids, weights)
    hidden, normed = norm(place, residual, norm_gain.reshape(1, WIDTH), sum_to_owner(partial))

    gate_up, down_proj, normed = tie(gate_up, down_proj, normed)
    piece = pack(chosen[1].reshape(1), gate_up, pick(down_proj, 1))
    (piece, send, mix), gathered = gather(normed, (piece, send, mix))
    outgoing = dispatch(send, gathered)
    second = send_weights(piece, 1)
    mine = lax.all_to_all(outgoing, ("prompt", "xh"), split_axis=0, concat_axis=0, tiled=True)
    other = lax.ppermute(mine, "core", SWAP)
    act_mine = open_experts(mine, up_first)
    act_other = open_experts(other, up_first)
    second, act_mine, act_other = tie(second, act_mine, act_other)
    done_other = close_experts(other, act_other, down_first, second)
    done_mine = close_experts(mine, act_mine, down_first, second)
    done = add(done_mine, lax.ppermute(done_other, "core", SWAP))
    back = lax.all_to_all(done, ("prompt", "xh"), split_axis=0, concat_axis=0, tiled=True)
    return finish(hidden, sum_to_owner(combine(mix, back)))


def solution(mesh):
    fine = Mesh(mesh.devices.reshape(8, 2, 2, 8), ("prompt", "xh", "core", "expert"))
    sample = ("prompt", "xh", "core")
    placed = (
        P(sample, None),
        P(sample, "expert"),
        P(sample, "expert", None),
        P("prompt", ("xh", "core"), "expert", None),
        P(sample),
        P("expert", None),
        P(),
        P(sample, None, "expert"),
        P(sample, "expert", None),
        P(sample, None),
        P(sample, None),
    )
    return jax.shard_map(
        shards,
        mesh=fine,
        in_specs=placed,
        out_specs=P((*sample, "expert"), None),
        check_vma=False,
    )
```

```python
import functools
import math

import jax
import jax.numpy as jnp
from jax import lax
from jax.experimental import pallas as pl
from jax.experimental.pallas import tpu as pltpu
from jax.sharding import Mesh, PartitionSpec as P

F32 = jnp.float32
BF16 = jnp.bfloat16
ROWS = 256
CHUNK = 32
PIECES = (0, 32, 64, 96, 128, 144, 160, 192, 224, 256)
WIDTH = 2880
WIDE = 2944
HEAD = 64
CAP = 20
PAD_CAP = 24
CHIPS = 16
SLOTS = CHIPS * PAD_CAP
KEY_BLOCK = 1024
UP_ROWS = 368
UNITS = 192
VMEM_LIMIT = 24 * 1024 * 1024
COLUMN_CUTS = ((0, 768), (768, 1536), (1536, 2304), (2304, 2880))


def params(count=0):
    if count:
        return pltpu.CompilerParams(
            vmem_limit_bytes=VMEM_LIMIT, dimension_semantics=("arbitrary",) * count
        )
    return pltpu.CompilerParams(vmem_limit_bytes=VMEM_LIMIT)


def spill(part, outs, low, high):
    part = part.astype(BF16)
    for out, start, stop in zip(outs, PIECES, PIECES[1:]):
        out[:, low:high] = part[start:stop]


PIECE_SHAPES = [(stop - start, WIDTH) for start, stop in zip(PIECES, PIECES[1:])]


def whole(shape):
    return pl.BlockSpec(shape, lambda *_: (0,) * len(shape))


def spread_cache(kv, keys_ref, even_ref, odd_ref, start):
    rows = kv.shape[0]
    wide = kv.astype(F32)
    turned = pltpu.roll(wide, HEAD, 1)
    first = lax.broadcasted_iota(jnp.int32, wide.shape, 1) < HEAD
    keys_ref[pl.ds(start, rows), :] = jnp.where(first, wide, turned).astype(BF16)
    even_ref[pl.ds(start, rows), :] = jnp.where(first, turned, 1.0).astype(BF16)
    odd_ref[pl.ds(start, rows), :] = jnp.where(first, 1.0, wide).astype(BF16)


def spread_queries(block):
    scaled = block.astype(F32) * (HEAD ** -0.5 * math.log2(math.e))
    high = scaled.astype(BF16).astype(F32)
    low = scaled - high
    first = lax.broadcasted_iota(jnp.int32, scaled.shape, 1) < HEAD
    even = jnp.where(first, high, pltpu.roll(low, HEAD, 1)).astype(BF16)
    odd = jnp.where(first, pltpu.roll(high, HEAD, 1), low).astype(BF16)
    return even, odd


def scores_of(queries, keys):
    return lax.dot_general(
        queries, keys, (((1,), (1,)), ((), ())), preferred_element_type=F32
    )


def attend(pair, keys_ref, values, cuts, states, allowed):
    items = [(side, start, size) for side in range(2) for start, size in cuts]

    def scores(side, start, size):
        found = scores_of(pair[side], keys_ref[start : start + size, :])
        if allowed is not None and start == 0:
            found = jnp.where(allowed, found, -1e30)
        return found

    ahead = scores(*items[0])
    for n, (side, start, size) in enumerate(items):
        here, ahead = ahead, scores(*items[n + 1]) if n + 1 < len(items) else None
        top, total = states[side]
        new_top = jnp.max(here, axis=1, keepdims=True)
        if top is not None:
            new_top = jnp.maximum(top, new_top)
        raised = jnp.exp2(here - new_top).astype(BF16)
        part = jnp.dot(
            raised, values[side][start : start + size, :], preferred_element_type=F32
        )
        if top is not None:
            part = part + total * jnp.exp2(top - new_top)
        states[side] = (new_top, part)
    return states


def first_kernel(
    length_ref, q_ref, resp_ref, own_ref, near_ref, top_ref, total_ref, keys, even, odd
):
    piece = own_ref.shape[0]

    @pl.when(pl.program_id(0) == 0)
    def _():
        spread_cache(resp_ref[...], keys, even, odd, 0)
        spread_cache(own_ref[...], keys, even, odd, ROWS)
        spread_cache(near_ref[...], keys, even, odd, ROWS + piece)

    row = lax.broadcasted_iota(jnp.int32, (ROWS, ROWS), 0)
    col = lax.broadcasted_iota(jnp.int32, (ROWS, ROWS), 1)
    allowed = (col <= row) & (col < length_ref[0])
    cuts = [(0, ROWS)] + [
        (ROWS + start, KEY_BLOCK) for start in range(0, 2 * piece, KEY_BLOCK)
    ]
    pair = spread_queries(q_ref[...])
    states = attend(pair, keys, (even, odd), cuts, [(None, None)] * 2, allowed)
    for side, (top, total) in enumerate(states):
        top_ref[side] = jnp.broadcast_to(top, (ROWS, 2 * HEAD))
        total_ref[side] = total


def second_kernel(
    place_ref, q_ref, a_ref, b_ref, top_ref, total_ref, proj_ref, *rest
):
    outs, (keys, even, odd, attended, turned) = rest[:9], rest[9:]
    piece = a_ref.shape[0]
    step = pl.program_id(0)

    @pl.when(step == 0)
    def _():
        spread_cache(a_ref[...], keys, even, odd, 0)
        spread_cache(b_ref[...], keys, even, odd, piece)

    cuts = [(start, KEY_BLOCK) for start in range(0, 2 * piece, KEY_BLOCK)]
    pair = spread_queries(q_ref[...])
    states = [(top_ref[side][:, :1], total_ref[side]) for side in range(2)]
    states = attend(pair, keys, (even, odd), cuts, states, None)
    totals = [total for _, total in states]
    first = lax.broadcasted_iota(jnp.int32, (ROWS, 2 * HEAD), 1) < HEAD
    numerator = jnp.where(first, totals[0], totals[1])
    denominator = jnp.where(
        first, pltpu.roll(totals[0], HEAD, 1), pltpu.roll(totals[1], HEAD, 1)
    )
    attended[step] = (numerator / denominator).astype(BF16)

    @pl.when(step == pl.num_programs(0) - 1)
    def _():
        for k in range(8):
            source = pl.multiple_of(lax.rem(place_ref[0] + k, 8) * CHUNK, CHUNK)
            for j in range(4):
                turned[CHUNK * k : CHUNK * (k + 1), 128 * j : 128 * (j + 1)] = attended[
                    j, pl.ds(source, CHUNK), :
                ]
        rows = turned[...]
        for low, high in COLUMN_CUTS:
            spill(scores_of(rows, proj_ref[low:high, :]), outs, low, high)


QUERY_SPEC = pl.BlockSpec((ROWS, 2 * HEAD), lambda i: (0, i))
STATE_SPEC = pl.BlockSpec((2, ROWS, 2 * HEAD), lambda i: (i, 0, 0))


def spread_scratch(rows):
    return [pltpu.VMEM((rows, 2 * HEAD), BF16)] * 3


def attend_cost(piece):
    return pl.CostEstimate(
        flops=8 * ROWS * 4 * 2 * HEAD * 2 * piece,
        bytes_accessed=5 << 20,
        transcendentals=8 * ROWS * 2 * piece,
    )


def attend_near(lengths, queries, response, own, near):
    pairs = queries.shape[1] // (2 * HEAD)
    piece = own.shape[0]
    state = (2 * pairs, ROWS, 2 * HEAD)
    return pl.pallas_call(
        first_kernel,
        grid=(pairs,),
        in_specs=[
            pl.BlockSpec(memory_space=pltpu.SMEM),
            QUERY_SPEC,
            whole((ROWS, 2 * HEAD)),
            whole((piece, 2 * HEAD)),
            whole((piece, 2 * HEAD)),
        ],
        out_specs=[STATE_SPEC] * 2,
        out_shape=[jax.ShapeDtypeStruct(state, F32)] * 2,
        scratch_shapes=spread_scratch(ROWS + 2 * piece),
        compiler_params=params(1),
        cost_estimate=attend_cost(piece),
        name="attend_near",
    )(lengths, queries, response, own, near)


def attend_far(place, queries, far, far_near, top, total, out_proj):
    pairs = queries.shape[1] // (2 * HEAD)
    piece = far.shape[0]
    return pl.pallas_call(
        second_kernel,
        grid=(pairs,),
        in_specs=[
            pl.BlockSpec(memory_space=pltpu.SMEM),
            QUERY_SPEC,
            whole((piece, 2 * HEAD)),
            whole((piece, 2 * HEAD)),
            STATE_SPEC,
            STATE_SPEC,
            whole(out_proj.shape),
        ],
        out_specs=[whole(shape) for shape in PIECE_SHAPES],
        out_shape=[jax.ShapeDtypeStruct(shape, BF16) for shape in PIECE_SHAPES],
        scratch_shapes=spread_scratch(2 * piece)
        + [pltpu.VMEM((pairs, ROWS, 2 * HEAD), BF16), pltpu.VMEM((ROWS, queries.shape[1]), BF16)],
        compiler_params=params(1),
        cost_estimate=attend_cost(piece),
        name="attend_far",
    )(place, queries, far, far_near, top, total, out_proj)


def turned_columns(ref, turn):
    rows = ref[...].astype(F32)
    rows = jnp.concatenate([rows, jnp.zeros((8 - rows.shape[0], ROWS), F32)])
    return jnp.transpose(pltpu.roll(rows, turn, 1))


def routing_kernel(place_ref, ids_ref, weights_ref, send_ref, mix_ref):
    turn = lax.rem((8 - place_ref[0]) * CHUNK, ROWS)
    ids = turned_columns(ids_ref, turn).astype(jnp.int32)
    weights = turned_columns(weights_ref, turn)
    routes = ids_ref.shape[0]
    expert = lax.broadcasted_iota(jnp.int32, (ROWS, 128), 1)
    named = [ids[:, r : r + 1] == expert for r in range(routes)]
    count = sum(jnp.where(n, 1.0, 0.0) for n in named)
    row = lax.broadcasted_iota(jnp.int32, (ROWS, ROWS), 0)
    col = lax.broadcasted_iota(jnp.int32, (ROWS, ROWS), 1)
    earlier = jnp.dot(
        jnp.where(col < row, 1.0, 0.0).astype(BF16),
        count.astype(BF16),
        preferred_element_type=F32,
    )
    slot = lax.broadcasted_iota(jnp.int32, (ROWS, SLOTS), 1)
    group = lax.rem(place_ref[0], 4)
    send = jnp.zeros((ROWS, SLOTS), F32)
    mix = jnp.zeros((ROWS, SLOTS), F32)
    for r in range(routes):
        rank = jnp.sum(jnp.where(named[r], earlier, 0.0), axis=1, keepdims=True)
        chosen = ids[:, r : r + 1]
        chip = lax.shift_right_logical(chosen, 2)
        mine = lax.bitwise_and(chosen, 3) == group
        at = jnp.where(mine, chip * PAD_CAP + rank.astype(jnp.int32), -1)
        hit = slot == at
        send = send + jnp.where(hit, 1.0, 0.0)
        mix = mix + jnp.where(hit, weights[:, r : r + 1], 0.0)
    send_ref[...] = jnp.transpose(send).astype(BF16)
    high = mix.astype(BF16)
    mix_ref[:, :SLOTS] = high
    mix_ref[:, SLOTS:] = (mix - high.astype(F32)).astype(BF16)


def routing(place, ids, weights):
    return pl.pallas_call(
        routing_kernel,
        in_specs=[
            pl.BlockSpec(memory_space=pltpu.SMEM),
            whole(ids.shape),
            whole(weights.shape),
        ],
        grid=(1,),
        out_specs=[whole((SLOTS, ROWS)), whole((ROWS, 2 * SLOTS))],
        out_shape=[
            jax.ShapeDtypeStruct((SLOTS, ROWS), BF16),
            jax.ShapeDtypeStruct((ROWS, 2 * SLOTS), BF16),
        ],
        compiler_params=params(1),
        name="routing",
    )(place, ids, weights)


def own_rows_kernel(place_ref, columns_ref, out_ref):
    row = lax.broadcasted_iota(jnp.int32, (CHUNK, ROWS), 0)
    col = lax.broadcasted_iota(jnp.int32, (CHUNK, ROWS), 1)
    pick = jnp.where(col == row + place_ref[0] * CHUNK, 1.0, 0.0).astype(BF16)
    for low, high in COLUMN_CUTS:
        out_ref[:, low:high] = scores_of(pick, columns_ref[low:high, :]).astype(BF16)


def own_rows(place, columns):
    return pl.pallas_call(
        own_rows_kernel,
        grid=(1,),
        in_specs=[pl.BlockSpec(memory_space=pltpu.SMEM), whole(columns.shape)],
        out_specs=whole((CHUNK, WIDTH)),
        out_shape=jax.ShapeDtypeStruct((CHUNK, WIDTH), BF16),
        compiler_params=params(1),
        name="own_rows",
    )(place, columns)


def norm_kernel(residual_ref, gain_ref, *refs):
    parts, (hidden_ref, normed_ref) = refs[:5], refs[5:]
    projected = parts[0][...].astype(F32)
    for part in parts[1:]:
        projected = projected + part[...].astype(F32)
    hidden = residual_ref[...].astype(F32) + projected
    inverse = lax.rsqrt(jnp.mean(hidden * hidden, axis=1, keepdims=True) + 1e-5)
    hidden_ref[...] = hidden
    normed_ref[...] = (hidden * inverse * gain_ref[...]).astype(BF16)


def norm(residual, gain, parts):
    chunk = (CHUNK, WIDTH)
    return pl.pallas_call(
        norm_kernel,
        grid=(1,),
        in_specs=[whole(chunk), whole((1, WIDTH))] + [whole(chunk)] * len(parts),
        out_specs=[whole(chunk)] * 2,
        out_shape=[jax.ShapeDtypeStruct(chunk, F32), jax.ShapeDtypeStruct(chunk, BF16)],
        compiler_params=params(1),
        name="norm",
    )(residual, gain, *parts)


def dispatch_kernel(send_ref, *refs):
    parts, (out_ref, rows) = refs[:9], refs[9:]
    for part, start, stop in zip(parts, PIECES, PIECES[1:]):
        rows[start:stop, :] = part[...]
    for low, high in COLUMN_CUTS:
        out_ref[:, low:high] = jnp.dot(
            send_ref[...], rows[:, low:high], preferred_element_type=F32
        ).astype(BF16)


def dispatch(send, parts):
    return pl.pallas_call(
        dispatch_kernel,
        grid=(1,),
        in_specs=[whole(send.shape)] + [whole(shape) for shape in PIECE_SHAPES],
        out_specs=whole((SLOTS, WIDE)),
        out_shape=jax.ShapeDtypeStruct((SLOTS, WIDE), BF16),
        scratch_shapes=[pltpu.VMEM((ROWS, WIDTH), BF16)],
        compiler_params=params(1),
        name="dispatch",
    )(send, *parts)


def combine_kernel(mix_ref, back_ref, *outs):
    for low, high in COLUMN_CUTS:
        block = back_ref[:, low:high]
        part = jnp.dot(mix_ref[:, :SLOTS], block, preferred_element_type=F32)
        part = part + jnp.dot(mix_ref[:, SLOTS:], block, preferred_element_type=F32)
        spill(part, outs, low, high)


def combine(mix, back):
    return pl.pallas_call(
        combine_kernel,
        grid=(1,),
        in_specs=[whole(mix.shape), whole(back.shape)],
        out_specs=[whole(shape) for shape in PIECE_SHAPES],
        out_shape=[jax.ShapeDtypeStruct(shape, BF16) for shape in PIECE_SHAPES],
        compiler_params=params(1),
        name="combine",
    )(mix, back)


def finish_kernel(hidden_ref, *refs):
    parts, out_ref = refs[:5], refs[5]
    total = parts[0][...].astype(F32)
    for part in parts[1:]:
        total = total + part[...].astype(F32)
    out_ref[...] = (hidden_ref[...] + total).astype(BF16)


def finish(hidden, parts):
    return pl.pallas_call(
        finish_kernel,
        grid=(1,),
        in_specs=[whole((CHUNK, WIDTH))] * 6,
        out_specs=whole((CHUNK, WIDTH)),
        out_shape=jax.ShapeDtypeStruct((CHUNK, WIDTH), BF16),
        compiler_params=params(1),
        name="finish",
    )(hidden, *parts)


def pack_kernel(_, up_ref, down_ref, out_ref):
    double, units = up_ref.shape[1], down_ref.shape[0]
    pad = jnp.zeros((UP_ROWS - double, WIDTH), BF16)
    out_ref[:UP_ROWS, :] = jnp.concatenate([up_ref[0], pad])
    pad = jnp.zeros((UNITS - units, WIDTH), BF16)
    out_ref[UP_ROWS:, :] = jnp.concatenate([down_ref[...], pad])


def pack(local, ups, down):
    shape = (UP_ROWS + UNITS, WIDTH)
    return pl.pallas_call(
        pack_kernel,
        grid_spec=pltpu.PrefetchScalarGridSpec(
            num_scalar_prefetch=1,
            grid=(1,),
            in_specs=[
                pl.BlockSpec((1, *ups.shape[1:]), lambda i, local: (local[0], 0, 0)),
                pl.BlockSpec(down.shape, lambda i, local: (0, 0)),
            ],
            out_specs=pl.BlockSpec(shape, lambda i, local: (0, 0)),
        ),
        out_shape=jax.ShapeDtypeStruct(shape, BF16),
        compiler_params=params(1),
        name="pack",
    )(local, ups, down)


def activation(x, rows, units):
    shape = (rows.shape[0], units)
    row = lax.broadcasted_iota(jnp.int32, shape, 0)
    col = lax.broadcasted_iota(jnp.int32, shape, 1)
    pick = jnp.where(row == 2 * col, 1.0, 0.0).astype(BF16)
    both = scores_of(x, rows)
    up = jnp.concatenate([both[:, 1:], both[:, :1]], axis=1)
    act = ((up + 1.0) * both * jax.nn.sigmoid(1.702 * both)).astype(BF16)
    return jnp.dot(act, pick, preferred_element_type=F32).astype(BF16)


def open_kernel(x_ref, up_ref, down_ref, out_ref):
    act = activation(x_ref[:, :WIDTH], up_ref[...], down_ref.shape[0])
    for low, high in COLUMN_CUTS:
        part = jnp.dot(act, down_ref[:, low:high], preferred_element_type=F32)
        out_ref[:, low:high] = part.astype(BF16)


def close_kernel(x_ref, half_ref, piece_ref, out_ref):
    act = activation(x_ref[:, :WIDTH], piece_ref[:UP_ROWS, :], UNITS)
    for low, high in COLUMN_CUTS:
        total = half_ref[:, low:high].astype(F32)
        total = total + jnp.dot(
            act, piece_ref[UP_ROWS:, low:high], preferred_element_type=F32
        )
        out_ref[:, low:high] = total.astype(out_ref.dtype)


def expert_cost(rows, flops):
    return pl.CostEstimate(
        flops=rows * flops, bytes_accessed=6 << 20, transcendentals=rows * 360
    )


def open_experts(x, up, down):
    shape = (x.shape[0], WIDE)
    return pl.pallas_call(
        open_kernel,
        grid=(1,),
        in_specs=[whole(x.shape), whole(up.shape), whole(down.shape)],
        out_specs=whole(shape),
        out_shape=jax.ShapeDtypeStruct(shape, BF16),
        compiler_params=params(1),
        cost_estimate=expert_cost(shape[0], WIDTH * 720),
        name="open_experts",
    )(x, up, down)


def close_experts(x, act, piece):
    rows = x.shape[0]
    return pl.pallas_call(
        close_kernel,
        grid=(1,),
        in_specs=[whole(w.shape) for w in (x, act, piece)],
        out_specs=whole((rows, WIDE)),
        out_shape=jax.ShapeDtypeStruct((rows, WIDE), BF16),
        compiler_params=params(1),
        cost_estimate=expert_cost(rows, WIDTH * 1440),
        name="close_experts",
    )(x, act, piece)


MOVES = (
    ((0, 8), (1, 0), (7, 9), (2, 1), (10, 2), (11, 10), (9, 3), (12, 11))
    + ((5, 12), (3, 4), (6, 13), (4, 5), (8, 6), (13, 14), (15, 7), (14, 15)),
    ((7, 8), (2, 0), (1, 9), (0, 1), (9, 2), (12, 10), (11, 3), (10, 11))
    + ((4, 12), (6, 4), (5, 13), (3, 5), (14, 6), (15, 14), (13, 7), (8, 15)),
)
SENT = tuple(sum((goal % 2) << source for source, goal in moves) for moves in MOVES)


def shift(step):
    return [(i, (i + step) % 8) for i in range(8)]


def tie(*values):
    return lax.optimization_barrier(values)


def add(a, b):
    return (a.astype(F32) + b.astype(F32)).astype(BF16)


def move(chunk, step):
    return lax.ppermute(chunk, "expert", shift(step))


def join_kernel(*refs):
    for side in range(2):
        own, whole_ref, half, out = refs[3 * side : 3 * side + 3] + (refs[6 + side],)
        rows = slice(side * CHUNK // 2, (side + 1) * CHUNK // 2)
        rest = slice((1 - side) * CHUNK // 2, (2 - side) * CHUNK // 2)
        total = own[...].astype(F32) + whole_ref[...].astype(F32)
        out[rest, :] = total[rest].astype(BF16)
        out[rows, :] = (total[rows] + half[...].astype(F32)).astype(BF16)


def join(*parts):
    return pl.pallas_call(
        join_kernel,
        grid=(1,),
        in_specs=[whole(part.shape) for part in parts],
        out_specs=[whole((CHUNK, WIDTH))] * 2,
        out_shape=[jax.ShapeDtypeStruct((CHUNK, WIDTH), BF16)] * 2,
        compiler_params=params(1),
        name="join",
    )(*parts)


def sum_to_owner(parts):
    own, up_1, up_2, up_3, half_down, half_up, down_3, down_2, down_1 = parts
    down, up = join(
        down_2, move(down_3, -1), move(half_down, -2), up_2, move(up_3, 1), move(half_up, 2)
    )
    return [own, move(down_1, -1), move(up_1, 1), move(down, -2), move(up, 2)]


def gather(mine, beside):
    near = move(mine, -1), move(mine, 1)
    *beside, after, before = tie(*beside, move(mine, -2), move(mine, 2))
    half = CHUNK // 2
    far = move(after[:half], -2), move(before[half:], 2)
    third, fifth = move(after, -1), move(before, 1)
    return beside, [mine, near[0], after, third, *far, fifth, before, near[1]]


SWAP = [(0, 1), (1, 0)]


def shards(
    residual,
    queries,
    response_key_value,
    prompt_cache,
    lengths,
    out_proj,
    norm_gain,
    gate_up,
    down_proj,
    expert_ids,
    gate_weights,
):
    z = lax.axis_index("expert")
    core = lax.axis_index("core")
    place = z.astype(jnp.int32).reshape(1)

    own = prompt_cache.reshape(prompt_cache.shape[1], 2 * HEAD)
    near = lax.ppermute(own, "core", SWAP)
    far = lax.ppermute(own, "xh", SWAP)

    gate_up = jnp.transpose(gate_up, (0, 2, 1))
    device = core * 8 + z
    chosen = [
        lax.bitwise_and(lax.shift_right_logical(jnp.int32(table), device), 1) for table in SENT
    ]

    def send_weights(piece, n):
        return lax.ppermute(piece, ("core", "expert"), MOVES[n])

    def pick(array, n):
        return lax.dynamic_index_in_dim(array, chosen[n], 0, keepdims=False)

    up, near = tie(pick(gate_up, 0), near)
    up_first = send_weights(up, 0)
    response = response_key_value.reshape(ROWS, 2 * HEAD)
    top, total = attend_near(lengths, queries, response, own, near)

    down, far, top = tie(pick(down_proj, 0), far, top)
    down_first = send_weights(down, 0)
    far_near = lax.ppermute(far, "core", SWAP)
    partial = attend_far(place, queries, far, far_near, top, total, out_proj.T)
    up_first, down_first, *partial = tie(up_first, down_first, *partial)

    ids, weights, residual, partial[0] = tie(
        expert_ids.T, gate_weights.T, residual.T, partial[0]
    )
    send, mix = routing(place, ids, weights)
    residual = own_rows(place, residual)
    hidden, normed = norm(residual, norm_gain.reshape(1, WIDTH), sum_to_owner(partial))

    gate_up, down_proj, normed = tie(gate_up, down_proj, normed)
    piece = pack(chosen[1].reshape(1), gate_up, pick(down_proj, 1))
    (piece, send, mix), gathered = gather(normed, (piece, send, mix))
    outgoing = dispatch(send, gathered)
    second = send_weights(piece, 1)
    mine = lax.all_to_all(outgoing, ("prompt", "xh"), split_axis=0, concat_axis=0, tiled=True)
    other = lax.ppermute(mine, "core", SWAP)
    act_mine = open_experts(mine, up_first, down_first)
    act_other = open_experts(other, up_first, down_first)
    second, act_mine, act_other = tie(second, act_mine, act_other)
    done_other = close_experts(other, act_other, second)
    done_mine = close_experts(mine, act_mine, second)
    done = add(done_mine, lax.ppermute(done_other, "core", SWAP))
    back = lax.all_to_all(done, ("prompt", "xh"), split_axis=0, concat_axis=0, tiled=True)
    return finish(hidden, sum_to_owner(combine(mix, back)))


def solution(mesh):
    fine = Mesh(mesh.devices.reshape(8, 2, 2, 8), ("prompt", "xh", "core", "expert"))
    sample = ("prompt", "xh", "core")
    placed = (
        P(sample, None),
        P(sample, "expert"),
        P(sample, "expert", None),
        P("prompt", ("xh", "core"), "expert", None),
        P(sample),
        P("expert", None),
        P(),
        P(sample, None, "expert"),
        P(sample, "expert", None),
        P(sample, None),
        P(sample, None),
    )
    return jax.shard_map(
        shards,
        mesh=fine,
        in_specs=placed,
        out_specs=P((*sample, "expert"), None),
        check_vma=False,
    )
```

```python
import functools
import math

import jax
import jax.numpy as jnp
from jax import lax
from jax.experimental import pallas as pl
from jax.experimental.pallas import tpu as pltpu
from jax.sharding import Mesh, PartitionSpec as P

F32 = jnp.float32
BF16 = jnp.bfloat16
ROWS = 256
CHUNK = 32
PIECES = (0, 32, 64, 96, 128, 144, 160, 192, 224, 256)
WIDTH = 2880
WIDE = 2944
HEAD = 64
CAP = 20
PAD_CAP = 24
CHIPS = 16
SLOTS = CHIPS * PAD_CAP
KEY_BLOCK = 2048
UP_ROWS = 368
UNITS = 192
VMEM_LIMIT = 24 * 1024 * 1024
COLUMN_CUTS = ((0, 768), (768, 1536), (1536, 2304), (2304, 2880))


def params(count=0):
    if count:
        return pltpu.CompilerParams(
            vmem_limit_bytes=VMEM_LIMIT, dimension_semantics=("arbitrary",) * count
        )
    return pltpu.CompilerParams(vmem_limit_bytes=VMEM_LIMIT)


def spill(part, outs, low, high):
    part = part.astype(BF16)
    for out, start, stop in zip(outs, PIECES, PIECES[1:]):
        out[:, low:high] = part[start:stop]


PIECE_SHAPES = [(stop - start, WIDTH) for start, stop in zip(PIECES, PIECES[1:])]


def whole(shape):
    return pl.BlockSpec(shape, lambda *_: (0,) * len(shape))


def spread_cache(kv, keys_ref, even_ref, odd_ref, start):
    rows = kv.shape[0]
    wide = kv.astype(F32)
    turned = pltpu.roll(wide, HEAD, 1)
    first = lax.broadcasted_iota(jnp.int32, wide.shape, 1) < HEAD
    keys_ref[pl.ds(start, rows), :] = jnp.where(first, wide, turned).astype(BF16)
    even_ref[pl.ds(start, rows), :] = jnp.where(first, turned, 1.0).astype(BF16)
    odd_ref[pl.ds(start, rows), :] = jnp.where(first, 1.0, wide).astype(BF16)


def spread_queries(block):
    scaled = block.astype(F32) * (HEAD ** -0.5 * math.log2(math.e))
    high = scaled.astype(BF16).astype(F32)
    low = scaled - high
    first = lax.broadcasted_iota(jnp.int32, scaled.shape, 1) < HEAD
    even = jnp.where(first, high, pltpu.roll(low, HEAD, 1)).astype(BF16)
    odd = jnp.where(first, pltpu.roll(high, HEAD, 1), low).astype(BF16)
    return even, odd


def scores_of(queries, keys):
    return lax.dot_general(
        queries, keys, (((1,), (1,)), ((), ())), preferred_element_type=F32
    )


def attend(pair, keys_ref, values, cuts, states, allowed):
    items = [(side, start, size) for side in range(2) for start, size in cuts]

    def scores(side, start, size):
        found = scores_of(pair[side], keys_ref[start : start + size, :])
        if allowed is not None and start == 0:
            found = jnp.where(allowed, found, -1e30)
        return found

    ahead = scores(*items[0])
    for n, (side, start, size) in enumerate(items):
        here, ahead = ahead, scores(*items[n + 1]) if n + 1 < len(items) else None
        top, total = states[side]
        new_top = jnp.max(here, axis=1, keepdims=True)
        if top is not None:
            new_top = jnp.maximum(top, new_top)
        raised = jnp.exp2(here - new_top).astype(BF16)
        part = jnp.dot(
            raised, values[side][start : start + size, :], preferred_element_type=F32
        )
        if top is not None:
            part = part + total * jnp.exp2(top - new_top)
        states[side] = (new_top, part)
    return states


def first_kernel(
    length_ref, q_ref, resp_ref, own_ref, near_ref, top_ref, total_ref, keys, even, odd
):
    piece = own_ref.shape[0]

    @pl.when(pl.program_id(0) == 0)
    def _():
        spread_cache(resp_ref[...], keys, even, odd, 0)
        spread_cache(own_ref[...], keys, even, odd, ROWS)
        spread_cache(near_ref[...], keys, even, odd, ROWS + piece)

    row = lax.broadcasted_iota(jnp.int32, (ROWS, ROWS), 0)
    col = lax.broadcasted_iota(jnp.int32, (ROWS, ROWS), 1)
    allowed = (col <= row) & (col < length_ref[0])
    cuts = [(0, ROWS)] + [
        (ROWS + start, KEY_BLOCK) for start in range(0, 2 * piece, KEY_BLOCK)
    ]
    pair = spread_queries(q_ref[...])
    states = attend(pair, keys, (even, odd), cuts, [(None, None)] * 2, allowed)
    for side, (top, total) in enumerate(states):
        top_ref[side] = jnp.broadcast_to(top, (ROWS, 2 * HEAD))
        total_ref[side] = total


def second_kernel(
    place_ref, q_ref, a_ref, b_ref, top_ref, total_ref, proj_ref, *rest
):
    outs, (keys, even, odd, attended, turned) = rest[:9], rest[9:]
    piece = a_ref.shape[0]
    step = pl.program_id(0)

    @pl.when(step == 0)
    def _():
        spread_cache(a_ref[...], keys, even, odd, 0)
        spread_cache(b_ref[...], keys, even, odd, piece)

    cuts = [(start, KEY_BLOCK) for start in range(0, 2 * piece, KEY_BLOCK)]
    pair = spread_queries(q_ref[...])
    states = [(top_ref[side][:, :1], total_ref[side]) for side in range(2)]
    states = attend(pair, keys, (even, odd), cuts, states, None)
    totals = [total for _, total in states]
    first = lax.broadcasted_iota(jnp.int32, (ROWS, 2 * HEAD), 1) < HEAD
    numerator = jnp.where(first, totals[0], totals[1])
    denominator = jnp.where(
        first, pltpu.roll(totals[0], HEAD, 1), pltpu.roll(totals[1], HEAD, 1)
    )
    attended[step] = (numerator / denominator).astype(BF16)

    @pl.when(step == pl.num_programs(0) - 1)
    def _():
        for k in range(8):
            source = pl.multiple_of(lax.rem(place_ref[0] + k, 8) * CHUNK, CHUNK)
            for j in range(4):
                turned[CHUNK * k : CHUNK * (k + 1), 128 * j : 128 * (j + 1)] = attended[
                    j, pl.ds(source, CHUNK), :
                ]
        rows = turned[...]
        for low, high in COLUMN_CUTS:
            spill(scores_of(rows, proj_ref[low:high, :]), outs, low, high)


QUERY_SPEC = pl.BlockSpec((ROWS, 2 * HEAD), lambda i: (0, i))
STATE_SPEC = pl.BlockSpec((2, ROWS, 2 * HEAD), lambda i: (i, 0, 0))


def spread_scratch(rows):
    return [pltpu.VMEM((rows, 2 * HEAD), BF16)] * 3


def attend_cost(piece):
    return pl.CostEstimate(
        flops=8 * ROWS * 4 * 2 * HEAD * 2 * piece,
        bytes_accessed=5 << 20,
        transcendentals=8 * ROWS * 2 * piece,
    )


def attend_near(lengths, queries, response, own, near):
    pairs = queries.shape[1] // (2 * HEAD)
    piece = own.shape[0]
    state = (2 * pairs, ROWS, 2 * HEAD)
    return pl.pallas_call(
        first_kernel,
        grid=(pairs,),
        in_specs=[
            pl.BlockSpec(memory_space=pltpu.SMEM),
            QUERY_SPEC,
            whole((ROWS, 2 * HEAD)),
            whole((piece, 2 * HEAD)),
            whole((piece, 2 * HEAD)),
        ],
        out_specs=[STATE_SPEC] * 2,
        out_shape=[jax.ShapeDtypeStruct(state, F32)] * 2,
        scratch_shapes=spread_scratch(ROWS + 2 * piece),
        compiler_params=params(1),
        cost_estimate=attend_cost(piece),
        name="attend_near",
    )(lengths, queries, response, own, near)


def attend_far(place, queries, far, far_near, top, total, out_proj):
    pairs = queries.shape[1] // (2 * HEAD)
    piece = far.shape[0]
    return pl.pallas_call(
        second_kernel,
        grid=(pairs,),
        in_specs=[
            pl.BlockSpec(memory_space=pltpu.SMEM),
            QUERY_SPEC,
            whole((piece, 2 * HEAD)),
            whole((piece, 2 * HEAD)),
            STATE_SPEC,
            STATE_SPEC,
            whole(out_proj.shape),
        ],
        out_specs=[whole(shape) for shape in PIECE_SHAPES],
        out_shape=[jax.ShapeDtypeStruct(shape, BF16) for shape in PIECE_SHAPES],
        scratch_shapes=spread_scratch(2 * piece)
        + [pltpu.VMEM((pairs, ROWS, 2 * HEAD), BF16), pltpu.VMEM((ROWS, queries.shape[1]), BF16)],
        compiler_params=params(1),
        cost_estimate=attend_cost(piece),
        name="attend_far",
    )(place, queries, far, far_near, top, total, out_proj)


def turned_columns(ref, turn):
    rows = ref[...].astype(F32)
    rows = jnp.concatenate([rows, jnp.zeros((8 - rows.shape[0], ROWS), F32)])
    return jnp.transpose(pltpu.roll(rows, turn, 1))


def routing_kernel(place_ref, ids_ref, weights_ref, send_ref, mix_ref):
    turn = lax.rem((8 - place_ref[0]) * CHUNK, ROWS)
    ids = turned_columns(ids_ref, turn).astype(jnp.int32)
    weights = turned_columns(weights_ref, turn)
    routes = ids_ref.shape[0]
    expert = lax.broadcasted_iota(jnp.int32, (ROWS, 128), 1)
    named = [ids[:, r : r + 1] == expert for r in range(routes)]
    count = sum(jnp.where(n, 1.0, 0.0) for n in named)
    row = lax.broadcasted_iota(jnp.int32, (ROWS, ROWS), 0)
    col = lax.broadcasted_iota(jnp.int32, (ROWS, ROWS), 1)
    earlier = jnp.dot(
        jnp.where(col < row, 1.0, 0.0).astype(BF16),
        count.astype(BF16),
        preferred_element_type=F32,
    )
    slot = lax.broadcasted_iota(jnp.int32, (ROWS, SLOTS), 1)
    group = lax.rem(place_ref[0], 4)
    send = jnp.zeros((ROWS, SLOTS), F32)
    mix = jnp.zeros((ROWS, SLOTS), F32)
    for r in range(routes):
        rank = jnp.sum(jnp.where(named[r], earlier, 0.0), axis=1, keepdims=True)
        chosen = ids[:, r : r + 1]
        chip = lax.shift_right_logical(chosen, 2)
        mine = lax.bitwise_and(chosen, 3) == group
        at = jnp.where(mine, chip * PAD_CAP + rank.astype(jnp.int32), -1)
        hit = slot == at
        send = send + jnp.where(hit, 1.0, 0.0)
        mix = mix + jnp.where(hit, weights[:, r : r + 1], 0.0)
    send_ref[...] = jnp.transpose(send).astype(BF16)
    high = mix.astype(BF16)
    mix_ref[:, :SLOTS] = high
    mix_ref[:, SLOTS:] = (mix - high.astype(F32)).astype(BF16)


def routing(place, ids, weights):
    return pl.pallas_call(
        routing_kernel,
        in_specs=[
            pl.BlockSpec(memory_space=pltpu.SMEM),
            whole(ids.shape),
            whole(weights.shape),
        ],
        grid=(1,),
        out_specs=[whole((SLOTS, ROWS)), whole((ROWS, 2 * SLOTS))],
        out_shape=[
            jax.ShapeDtypeStruct((SLOTS, ROWS), BF16),
            jax.ShapeDtypeStruct((ROWS, 2 * SLOTS), BF16),
        ],
        compiler_params=params(1),
        name="routing",
    )(place, ids, weights)


def own_rows_kernel(place_ref, columns_ref, out_ref):
    row = lax.broadcasted_iota(jnp.int32, (CHUNK, ROWS), 0)
    col = lax.broadcasted_iota(jnp.int32, (CHUNK, ROWS), 1)
    pick = jnp.where(col == row + place_ref[0] * CHUNK, 1.0, 0.0).astype(BF16)
    for low, high in COLUMN_CUTS:
        out_ref[:, low:high] = scores_of(pick, columns_ref[low:high, :]).astype(BF16)


def own_rows(place, columns):
    return pl.pallas_call(
        own_rows_kernel,
        grid=(1,),
        in_specs=[pl.BlockSpec(memory_space=pltpu.SMEM), whole(columns.shape)],
        out_specs=whole((CHUNK, WIDTH)),
        out_shape=jax.ShapeDtypeStruct((CHUNK, WIDTH), BF16),
        compiler_params=params(1),
        name="own_rows",
    )(place, columns)


def norm_kernel(residual_ref, gain_ref, *refs):
    parts, (hidden_ref, normed_ref) = refs[:5], refs[5:]
    projected = parts[0][...].astype(F32)
    for part in parts[1:]:
        projected = projected + part[...].astype(F32)
    hidden = residual_ref[...].astype(F32) + projected
    inverse = lax.rsqrt(jnp.mean(hidden * hidden, axis=1, keepdims=True) + 1e-5)
    hidden_ref[...] = hidden
    normed_ref[...] = (hidden * inverse * gain_ref[...]).astype(BF16)


def norm(residual, gain, parts):
    chunk = (CHUNK, WIDTH)
    return pl.pallas_call(
        norm_kernel,
        grid=(1,),
        in_specs=[whole(chunk), whole((1, WIDTH))] + [whole(chunk)] * len(parts),
        out_specs=[whole(chunk)] * 2,
        out_shape=[jax.ShapeDtypeStruct(chunk, F32), jax.ShapeDtypeStruct(chunk, BF16)],
        compiler_params=params(1),
        name="norm",
    )(residual, gain, *parts)


def dispatch_kernel(send_ref, *refs):
    parts, (out_ref, rows) = refs[:9], refs[9:]
    for part, start, stop in zip(parts, PIECES, PIECES[1:]):
        rows[start:stop, :] = part[...]
    for low, high in COLUMN_CUTS:
        out_ref[:, low:high] = jnp.dot(
            send_ref[...], rows[:, low:high], preferred_element_type=F32
        ).astype(BF16)


def dispatch(send, parts):
    return pl.pallas_call(
        dispatch_kernel,
        grid=(1,),
        in_specs=[whole(send.shape)] + [whole(shape) for shape in PIECE_SHAPES],
        out_specs=whole((SLOTS, WIDE)),
        out_shape=jax.ShapeDtypeStruct((SLOTS, WIDE), BF16),
        scratch_shapes=[pltpu.VMEM((ROWS, WIDTH), BF16)],
        compiler_params=params(1),
        name="dispatch",
    )(send, *parts)


def combine_kernel(chosen, mix_ref, back_ref, *outs):
    first, last = PIECES[chosen[0]], PIECES[chosen[-1] + 1]
    for low, high in COLUMN_CUTS:
        block = back_ref[:, low:high]
        part = jnp.dot(mix_ref[first:last, :SLOTS], block, preferred_element_type=F32)
        part = part + jnp.dot(mix_ref[first:last, SLOTS:], block, preferred_element_type=F32)
        part = part.astype(BF16)
        for out, k in zip(outs, chosen):
            out[:, low:high] = part[PIECES[k] - first : PIECES[k + 1] - first]


def combine_some(mix, back, chosen):
    shapes = [PIECE_SHAPES[k] for k in chosen]
    return pl.pallas_call(
        functools.partial(combine_kernel, chosen),
        grid=(1,),
        in_specs=[whole(mix.shape), whole(back.shape)],
        out_specs=[whole(shape) for shape in shapes],
        out_shape=[jax.ShapeDtypeStruct(shape, BF16) for shape in shapes],
        compiler_params=params(1),
        name="combine",
    )(mix, back)


def combine(mix, back):
    middle = combine_some(mix, back, (3, 4, 5, 6))
    rest = combine_some(mix, back, (0, 1, 2)), combine_some(mix, back, (7, 8))
    return [*rest[0], *middle, *rest[1]]


def finish_kernel(hidden_ref, *refs):
    parts, out_ref = refs[:5], refs[5]
    total = parts[0][...].astype(F32)
    for part in parts[1:]:
        total = total + part[...].astype(F32)
    out_ref[...] = (hidden_ref[...] + total).astype(BF16)


def finish(hidden, parts):
    return pl.pallas_call(
        finish_kernel,
        grid=(1,),
        in_specs=[whole((CHUNK, WIDTH))] * 6,
        out_specs=whole((CHUNK, WIDTH)),
        out_shape=jax.ShapeDtypeStruct((CHUNK, WIDTH), BF16),
        compiler_params=params(1),
        name="finish",
    )(hidden, *parts)


def pack_kernel(_, up_ref, down_ref, out_ref):
    double, units = up_ref.shape[1], down_ref.shape[0]
    pad = jnp.zeros((UP_ROWS - double, WIDTH), BF16)
    out_ref[:UP_ROWS, :] = jnp.concatenate([up_ref[0], pad])
    pad = jnp.zeros((UNITS - units, WIDTH), BF16)
    out_ref[UP_ROWS:, :] = jnp.concatenate([down_ref[...], pad])


def pack(local, ups, down):
    shape = (UP_ROWS + UNITS, WIDTH)
    return pl.pallas_call(
        pack_kernel,
        grid_spec=pltpu.PrefetchScalarGridSpec(
            num_scalar_prefetch=1,
            grid=(1,),
            in_specs=[
                pl.BlockSpec((1, *ups.shape[1:]), lambda i, local: (local[0], 0, 0)),
                pl.BlockSpec(down.shape, lambda i, local: (0, 0)),
            ],
            out_specs=pl.BlockSpec(shape, lambda i, local: (0, 0)),
        ),
        out_shape=jax.ShapeDtypeStruct(shape, BF16),
        compiler_params=params(1),
        name="pack",
    )(local, ups, down)


def activation(x, rows, units):
    shape = (rows.shape[0], units)
    row = lax.broadcasted_iota(jnp.int32, shape, 0)
    col = lax.broadcasted_iota(jnp.int32, shape, 1)
    pick = jnp.where(row == 2 * col, 1.0, 0.0).astype(BF16)
    both = scores_of(x, rows)
    up = jnp.concatenate([both[:, 1:], both[:, :1]], axis=1)
    act = ((up + 1.0) * both * jax.nn.sigmoid(1.702 * both)).astype(BF16)
    return jnp.dot(act, pick, preferred_element_type=F32).astype(BF16)


def open_kernel(x_ref, up_ref, down_ref, out_ref):
    act = activation(x_ref[:, :WIDTH], up_ref[...], down_ref.shape[0])
    for low, high in COLUMN_CUTS:
        part = jnp.dot(act, down_ref[:, low:high], preferred_element_type=F32)
        out_ref[:, low:high] = part.astype(BF16)


def close_kernel(x_ref, half_ref, piece_ref, out_ref):
    act = activation(x_ref[:, :WIDTH], piece_ref[:UP_ROWS, :], UNITS)
    for low, high in COLUMN_CUTS:
        total = half_ref[:, low:high].astype(F32)
        total = total + jnp.dot(
            act, piece_ref[UP_ROWS:, low:high], preferred_element_type=F32
        )
        out_ref[:, low:high] = total.astype(out_ref.dtype)


def expert_cost(rows, flops):
    return pl.CostEstimate(
        flops=rows * flops, bytes_accessed=6 << 20, transcendentals=rows * 360
    )


def open_experts(x, up, down):
    shape = (x.shape[0], WIDE)
    return pl.pallas_call(
        open_kernel,
        grid=(1,),
        in_specs=[whole(x.shape), whole(up.shape), whole(down.shape)],
        out_specs=whole(shape),
        out_shape=jax.ShapeDtypeStruct(shape, BF16),
        compiler_params=params(1),
        cost_estimate=expert_cost(shape[0], WIDTH * 720),
        name="open_experts",
    )(x, up, down)


def close_experts(x, act, piece):
    rows = x.shape[0]
    return pl.pallas_call(
        close_kernel,
        grid=(1,),
        in_specs=[whole(w.shape) for w in (x, act, piece)],
        out_specs=whole((rows, WIDE)),
        out_shape=jax.ShapeDtypeStruct((rows, WIDE), BF16),
        compiler_params=params(1),
        cost_estimate=expert_cost(rows, WIDTH * 1440),
        name="close_experts",
    )(x, act, piece)


MOVES = (
    ((0, 8), (1, 0), (7, 9), (2, 1), (10, 2), (11, 10), (9, 3), (12, 11))
    + ((5, 12), (3, 4), (6, 13), (4, 5), (8, 6), (13, 14), (15, 7), (14, 15)),
    ((7, 8), (2, 0), (1, 9), (0, 1), (9, 2), (12, 10), (11, 3), (10, 11))
    + ((4, 12), (6, 4), (5, 13), (3, 5), (14, 6), (15, 14), (13, 7), (8, 15)),
)
SENT = tuple(sum((goal % 2) << source for source, goal in moves) for moves in MOVES)


def shift(step):
    return [(i, (i + step) % 8) for i in range(8)]


def tie(*values):
    return lax.optimization_barrier(values)


def add(a, b):
    return (a.astype(F32) + b.astype(F32)).astype(BF16)


def move(chunk, step):
    return lax.ppermute(chunk, "expert", shift(step))


def join_kernel(*refs):
    for side in range(2):
        own, whole_ref, half, out = refs[3 * side : 3 * side + 3] + (refs[6 + side],)
        rows = slice(side * CHUNK // 2, (side + 1) * CHUNK // 2)
        rest = slice((1 - side) * CHUNK // 2, (2 - side) * CHUNK // 2)
        total = own[...].astype(F32) + whole_ref[...].astype(F32)
        out[rest, :] = total[rest].astype(BF16)
        out[rows, :] = (total[rows] + half[...].astype(F32)).astype(BF16)


def join(*parts):
    return pl.pallas_call(
        join_kernel,
        grid=(1,),
        in_specs=[whole(part.shape) for part in parts],
        out_specs=[whole((CHUNK, WIDTH))] * 2,
        out_shape=[jax.ShapeDtypeStruct((CHUNK, WIDTH), BF16)] * 2,
        compiler_params=params(1),
        name="join",
    )(*parts)


def sum_to_owner(parts):
    own, up_1, up_2, up_3, half_down, half_up, down_3, down_2, down_1 = parts
    down, up = join(
        down_2, move(down_3, -1), move(half_down, -2), up_2, move(up_3, 1), move(half_up, 2)
    )
    return [own, move(down_1, -1), move(up_1, 1), move(down, -2), move(up, 2)]


def gather(mine, beside):
    near = move(mine, -1), move(mine, 1)
    *beside, after, before = tie(*beside, move(mine, -2), move(mine, 2))
    half = CHUNK // 2
    far = move(after[:half], -2), move(before[half:], 2)
    third, fifth = move(after, -1), move(before, 1)
    return beside, [mine, near[0], after, third, *far, fifth, before, near[1]]


SWAP = [(0, 1), (1, 0)]


def shards(
    residual,
    queries,
    response_key_value,
    prompt_cache,
    lengths,
    out_proj,
    norm_gain,
    gate_up,
    down_proj,
    expert_ids,
    gate_weights,
):
    z = lax.axis_index("expert")
    core = lax.axis_index("core")
    place = z.astype(jnp.int32).reshape(1)

    own = prompt_cache.reshape(prompt_cache.shape[1], 2 * HEAD)
    near = lax.ppermute(own, "core", SWAP)
    far = lax.ppermute(own, "xh", SWAP)

    gate_up = jnp.transpose(gate_up, (0, 2, 1))
    device = core * 8 + z
    chosen = [
        lax.bitwise_and(lax.shift_right_logical(jnp.int32(table), device), 1) for table in SENT
    ]

    def send_weights(piece, n):
        return lax.ppermute(piece, ("core", "expert"), MOVES[n])

    def pick(array, n):
        return lax.dynamic_index_in_dim(array, chosen[n], 0, keepdims=False)

    up, near = tie(pick(gate_up, 0), near)
    up_first = send_weights(up, 0)
    response = response_key_value.reshape(ROWS, 2 * HEAD)
    top, total = attend_near(lengths, queries, response, own, near)

    down, far, top = tie(pick(down_proj, 0), far, top)
    down_first = send_weights(down, 0)
    far_near = lax.ppermute(far, "core", SWAP)
    partial = attend_far(place, queries, far, far_near, top, total, out_proj.T)
    up_first, down_first, *partial = tie(up_first, down_first, *partial)

    ids, weights, residual, partial[0] = tie(
        expert_ids.T, gate_weights.T, residual.T, partial[0]
    )
    send, mix = routing(place, ids, weights)
    residual = own_rows(place, residual)
    hidden, normed = norm(residual, norm_gain.reshape(1, WIDTH), sum_to_owner(partial))

    gate_up, down_proj, normed = tie(gate_up, down_proj, normed)
    piece = pack(chosen[1].reshape(1), gate_up, pick(down_proj, 1))
    (piece, send, mix), gathered = gather(normed, (piece, send, mix))
    outgoing = dispatch(send, gathered)
    second = send_weights(piece, 1)
    mine = lax.all_to_all(outgoing, ("prompt", "xh"), split_axis=0, concat_axis=0, tiled=True)
    other = lax.ppermute(mine, "core", SWAP)
    act_mine = open_experts(mine, up_first, down_first)
    act_other = open_experts(other, up_first, down_first)
    second, act_mine, act_other = tie(second, act_mine, act_other)
    done_other = close_experts(other, act_other, second)
    done_mine = close_experts(mine, act_mine, second)
    done = add(done_mine, lax.ppermute(done_other, "core", SWAP))
    back = lax.all_to_all(done, ("prompt", "xh"), split_axis=0, concat_axis=0, tiled=True)
    return finish(hidden, sum_to_owner(combine(mix, back)))


def solution(mesh):
    fine = Mesh(mesh.devices.reshape(8, 2, 2, 8), ("prompt", "xh", "core", "expert"))
    sample = ("prompt", "xh", "core")
    placed = (
        P(sample, None),
        P(sample, "expert"),
        P(sample, "expert", None),
        P("prompt", ("xh", "core"), "expert", None),
        P(sample),
        P("expert", None),
        P(),
        P(sample, None, "expert"),
        P(sample, "expert", None),
        P(sample, None),
        P(sample, None),
    )
    return jax.shard_map(
        shards,
        mesh=fine,
        in_specs=placed,
        out_specs=P((*sample, "expert"), None),
        check_vma=False,
    )
```

```python
import functools
import math

import jax
import jax.numpy as jnp
from jax import lax
from jax.experimental import pallas as pl
from jax.experimental.pallas import tpu as pltpu
from jax.sharding import Mesh, PartitionSpec as P

F32 = jnp.float32
BF16 = jnp.bfloat16
ROWS = 256
CHUNK = 32
PIECES = (0, 32, 64, 96, 128, 144, 160, 192, 224, 256)
WIDTH = 2880
WIDE = 2944
HEAD = 64
CAP = 20
PAD_CAP = 24
CHIPS = 16
SLOTS = CHIPS * PAD_CAP
KEY_BLOCK = 2048
UP_ROWS = 368
UNITS = 192
VMEM_LIMIT = 24 * 1024 * 1024
COLUMN_CUTS = ((0, 768), (768, 1536), (1536, 2304), (2304, 2880))


def params(count=0):
    if count:
        return pltpu.CompilerParams(
            vmem_limit_bytes=VMEM_LIMIT, dimension_semantics=("arbitrary",) * count
        )
    return pltpu.CompilerParams(vmem_limit_bytes=VMEM_LIMIT)


def spill(part, outs, low, high):
    part = part.astype(BF16)
    for out, start, stop in zip(outs, PIECES, PIECES[1:]):
        out[:, low:high] = part[start:stop]


PIECE_SHAPES = [(stop - start, WIDTH) for start, stop in zip(PIECES, PIECES[1:])]


def whole(shape):
    return pl.BlockSpec(shape, lambda *_: (0,) * len(shape))


def spread_cache(kv, keys_ref, even_ref, odd_ref, start):
    rows = kv.shape[0]
    wide = kv.astype(F32)
    turned = pltpu.roll(wide, HEAD, 1)
    first = lax.broadcasted_iota(jnp.int32, wide.shape, 1) < HEAD
    keys_ref[pl.ds(start, rows), :] = jnp.where(first, wide, turned).astype(BF16)
    even_ref[pl.ds(start, rows), :] = jnp.where(first, turned, 1.0).astype(BF16)
    odd_ref[pl.ds(start, rows), :] = jnp.where(first, 1.0, wide).astype(BF16)


def spread_queries(block):
    scaled = block.astype(F32) * (HEAD ** -0.5 * math.log2(math.e))
    high = scaled.astype(BF16).astype(F32)
    low = scaled - high
    first = lax.broadcasted_iota(jnp.int32, scaled.shape, 1) < HEAD
    even = jnp.where(first, high, pltpu.roll(low, HEAD, 1)).astype(BF16)
    odd = jnp.where(first, pltpu.roll(high, HEAD, 1), low).astype(BF16)
    return even, odd


def scores_of(queries, keys):
    return lax.dot_general(
        queries, keys, (((1,), (1,)), ((), ())), preferred_element_type=F32
    )


def attend(pair, keys_ref, values, cuts, states, allowed):
    items = [(side, start, size) for side in range(2) for start, size in cuts]

    def scores(side, start, size):
        found = scores_of(pair[side], keys_ref[start : start + size, :])
        if allowed is not None and start == 0:
            found = jnp.where(allowed, found, -1e30)
        return found

    ahead = scores(*items[0])
    for n, (side, start, size) in enumerate(items):
        here, ahead = ahead, scores(*items[n + 1]) if n + 1 < len(items) else None
        top, total = states[side]
        new_top = jnp.max(here, axis=1, keepdims=True)
        if top is not None:
            new_top = jnp.maximum(top, new_top)
        raised = jnp.exp2(here - new_top).astype(BF16)
        part = jnp.dot(
            raised, values[side][start : start + size, :], preferred_element_type=F32
        )
        if top is not None:
            part = part + total * jnp.exp2(top - new_top)
        states[side] = (new_top, part)
    return states


def first_kernel(
    length_ref, q_ref, resp_ref, own_ref, near_ref, top_ref, total_ref, keys, even, odd
):
    piece = own_ref.shape[0]

    @pl.when(pl.program_id(0) == 0)
    def _():
        spread_cache(resp_ref[...], keys, even, odd, 0)
        spread_cache(own_ref[...], keys, even, odd, ROWS)
        spread_cache(near_ref[...], keys, even, odd, ROWS + piece)

    row = lax.broadcasted_iota(jnp.int32, (ROWS, ROWS), 0)
    col = lax.broadcasted_iota(jnp.int32, (ROWS, ROWS), 1)
    allowed = (col <= row) & (col < length_ref[0])
    cuts = [(0, ROWS)] + [
        (ROWS + start, KEY_BLOCK) for start in range(0, 2 * piece, KEY_BLOCK)
    ]
    pair = spread_queries(q_ref[...])
    states = attend(pair, keys, (even, odd), cuts, [(None, None)] * 2, allowed)
    for side, (top, total) in enumerate(states):
        top_ref[side] = jnp.broadcast_to(top, (ROWS, 2 * HEAD))
        total_ref[side] = total


def second_kernel(
    place_ref, q_ref, a_ref, b_ref, top_ref, total_ref, proj_ref, *rest
):
    outs, (keys, even, odd, attended, turned) = rest[:9], rest[9:]
    piece = a_ref.shape[0]
    step = pl.program_id(0)

    @pl.when(step == 0)
    def _():
        spread_cache(a_ref[...], keys, even, odd, 0)
        spread_cache(b_ref[...], keys, even, odd, piece)

    cuts = [(start, KEY_BLOCK) for start in range(0, 2 * piece, KEY_BLOCK)]
    pair = spread_queries(q_ref[...])
    states = [(top_ref[side][:, :1], total_ref[side]) for side in range(2)]
    states = attend(pair, keys, (even, odd), cuts, states, None)
    totals = [total for _, total in states]
    first = lax.broadcasted_iota(jnp.int32, (ROWS, 2 * HEAD), 1) < HEAD
    numerator = jnp.where(first, totals[0], totals[1])
    denominator = jnp.where(
        first, pltpu.roll(totals[0], HEAD, 1), pltpu.roll(totals[1], HEAD, 1)
    )
    attended[step] = (numerator / denominator).astype(BF16)

    @pl.when(step == pl.num_programs(0) - 1)
    def _():
        for k in range(8):
            source = pl.multiple_of(lax.rem(place_ref[0] + k, 8) * CHUNK, CHUNK)
            for j in range(4):
                turned[CHUNK * k : CHUNK * (k + 1), 128 * j : 128 * (j + 1)] = attended[
                    j, pl.ds(source, CHUNK), :
                ]
        rows = turned[...]
        for low, high in COLUMN_CUTS:
            spill(scores_of(rows, proj_ref[low:high, :]), outs, low, high)


QUERY_SPEC = pl.BlockSpec((ROWS, 2 * HEAD), lambda i: (0, i))
STATE_SPEC = pl.BlockSpec((2, ROWS, 2 * HEAD), lambda i: (i, 0, 0))


def spread_scratch(rows):
    return [pltpu.VMEM((rows, 2 * HEAD), BF16)] * 3


def attend_cost(piece):
    return pl.CostEstimate(
        flops=8 * ROWS * 4 * 2 * HEAD * 2 * piece,
        bytes_accessed=5 << 20,
        transcendentals=8 * ROWS * 2 * piece,
    )


def attend_near(lengths, queries, response, own, near):
    pairs = queries.shape[1] // (2 * HEAD)
    piece = own.shape[0]
    state = (2 * pairs, ROWS, 2 * HEAD)
    return pl.pallas_call(
        first_kernel,
        grid=(pairs,),
        in_specs=[
            pl.BlockSpec(memory_space=pltpu.SMEM),
            QUERY_SPEC,
            whole((ROWS, 2 * HEAD)),
            whole((piece, 2 * HEAD)),
            whole((piece, 2 * HEAD)),
        ],
        out_specs=[STATE_SPEC] * 2,
        out_shape=[jax.ShapeDtypeStruct(state, F32)] * 2,
        scratch_shapes=spread_scratch(ROWS + 2 * piece),
        compiler_params=params(1),
        cost_estimate=attend_cost(piece),
        name="attend_near",
    )(lengths, queries, response, own, near)


def attend_far(place, queries, far, far_near, top, total, out_proj):
    pairs = queries.shape[1] // (2 * HEAD)
    piece = far.shape[0]
    return pl.pallas_call(
        second_kernel,
        grid=(pairs,),
        in_specs=[
            pl.BlockSpec(memory_space=pltpu.SMEM),
            QUERY_SPEC,
            whole((piece, 2 * HEAD)),
            whole((piece, 2 * HEAD)),
            STATE_SPEC,
            STATE_SPEC,
            whole(out_proj.shape),
        ],
        out_specs=[whole(shape) for shape in PIECE_SHAPES],
        out_shape=[jax.ShapeDtypeStruct(shape, BF16) for shape in PIECE_SHAPES],
        scratch_shapes=spread_scratch(2 * piece)
        + [pltpu.VMEM((pairs, ROWS, 2 * HEAD), BF16), pltpu.VMEM((ROWS, queries.shape[1]), BF16)],
        compiler_params=params(1),
        cost_estimate=attend_cost(piece),
        name="attend_far",
    )(place, queries, far, far_near, top, total, out_proj)


def turned_columns(ref, turn):
    rows = ref[...].astype(F32)
    rows = jnp.concatenate([rows, jnp.zeros((8 - rows.shape[0], ROWS), F32)])
    return jnp.transpose(pltpu.roll(rows, turn, 1))


def routing_kernel(place_ref, ids_ref, weights_ref, send_ref, mix_ref):
    turn = lax.rem((8 - place_ref[0]) * CHUNK, ROWS)
    ids = turned_columns(ids_ref, turn).astype(jnp.int32)
    weights = turned_columns(weights_ref, turn)
    routes = ids_ref.shape[0]
    expert = lax.broadcasted_iota(jnp.int32, (ROWS, 128), 1)
    named = [ids[:, r : r + 1] == expert for r in range(routes)]
    count = sum(jnp.where(n, 1.0, 0.0) for n in named)
    row = lax.broadcasted_iota(jnp.int32, (ROWS, ROWS), 0)
    col = lax.broadcasted_iota(jnp.int32, (ROWS, ROWS), 1)
    earlier = jnp.dot(
        jnp.where(col < row, 1.0, 0.0).astype(BF16),
        count.astype(BF16),
        preferred_element_type=F32,
    )
    slot = lax.broadcasted_iota(jnp.int32, (ROWS, SLOTS), 1)
    group = lax.rem(place_ref[0], 4)
    send = jnp.zeros((ROWS, SLOTS), F32)
    mix = jnp.zeros((ROWS, SLOTS), F32)
    for r in range(routes):
        rank = jnp.sum(jnp.where(named[r], earlier, 0.0), axis=1, keepdims=True)
        chosen = ids[:, r : r + 1]
        chip = lax.shift_right_logical(chosen, 2)
        mine = lax.bitwise_and(chosen, 3) == group
        at = jnp.where(mine, chip * PAD_CAP + rank.astype(jnp.int32), -1)
        hit = slot == at
        send = send + jnp.where(hit, 1.0, 0.0)
        mix = mix + jnp.where(hit, weights[:, r : r + 1], 0.0)
    send_ref[...] = jnp.transpose(send).astype(BF16)
    high = mix.astype(BF16)
    mix_ref[:, :SLOTS] = high
    mix_ref[:, SLOTS:] = (mix - high.astype(F32)).astype(BF16)


def routing(place, ids, weights):
    return pl.pallas_call(
        routing_kernel,
        in_specs=[
            pl.BlockSpec(memory_space=pltpu.SMEM),
            whole(ids.shape),
            whole(weights.shape),
        ],
        grid=(1,),
        out_specs=[whole((SLOTS, ROWS)), whole((ROWS, 2 * SLOTS))],
        out_shape=[
            jax.ShapeDtypeStruct((SLOTS, ROWS), BF16),
            jax.ShapeDtypeStruct((ROWS, 2 * SLOTS), BF16),
        ],
        compiler_params=params(1),
        name="routing",
    )(place, ids, weights)


def own_rows_kernel(place_ref, columns_ref, out_ref):
    row = lax.broadcasted_iota(jnp.int32, (CHUNK, ROWS), 0)
    col = lax.broadcasted_iota(jnp.int32, (CHUNK, ROWS), 1)
    pick = jnp.where(col == row + place_ref[0] * CHUNK, 1.0, 0.0).astype(BF16)
    for low, high in COLUMN_CUTS:
        out_ref[:, low:high] = scores_of(pick, columns_ref[low:high, :]).astype(BF16)


def own_rows(place, columns):
    return pl.pallas_call(
        own_rows_kernel,
        grid=(1,),
        in_specs=[pl.BlockSpec(memory_space=pltpu.SMEM), whole(columns.shape)],
        out_specs=whole((CHUNK, WIDTH)),
        out_shape=jax.ShapeDtypeStruct((CHUNK, WIDTH), BF16),
        compiler_params=params(1),
        name="own_rows",
    )(place, columns)


def norm_kernel(residual_ref, gain_ref, *refs):
    parts, (hidden_ref, normed_ref) = refs[:5], refs[5:]
    projected = parts[0][...].astype(F32)
    for part in parts[1:]:
        projected = projected + part[...].astype(F32)
    hidden = residual_ref[...].astype(F32) + projected
    inverse = lax.rsqrt(jnp.mean(hidden * hidden, axis=1, keepdims=True) + 1e-5)
    hidden_ref[...] = hidden
    normed_ref[...] = (hidden * inverse * gain_ref[...]).astype(BF16)


def norm(residual, gain, parts):
    chunk = (CHUNK, WIDTH)
    return pl.pallas_call(
        norm_kernel,
        grid=(1,),
        in_specs=[whole(chunk), whole((1, WIDTH))] + [whole(chunk)] * len(parts),
        out_specs=[whole(chunk)] * 2,
        out_shape=[jax.ShapeDtypeStruct(chunk, F32), jax.ShapeDtypeStruct(chunk, BF16)],
        compiler_params=params(1),
        name="norm",
    )(residual, gain, *parts)


def dispatch_kernel(send_ref, *refs):
    parts, (out_ref, rows) = refs[:9], refs[9:]
    for part, start, stop in zip(parts, PIECES, PIECES[1:]):
        rows[start:stop, :] = part[...]
    for low, high in COLUMN_CUTS:
        out_ref[:, low:high] = jnp.dot(
            send_ref[...], rows[:, low:high], preferred_element_type=F32
        ).astype(BF16)


def dispatch(send, parts):
    return pl.pallas_call(
        dispatch_kernel,
        grid=(1,),
        in_specs=[whole(send.shape)] + [whole(shape) for shape in PIECE_SHAPES],
        out_specs=whole((SLOTS, WIDE)),
        out_shape=jax.ShapeDtypeStruct((SLOTS, WIDE), BF16),
        scratch_shapes=[pltpu.VMEM((ROWS, WIDTH), BF16)],
        compiler_params=params(1),
        name="dispatch",
    )(send, *parts)


def combine_kernel(chosen, mix_ref, back_ref, *outs):
    for low, high in COLUMN_CUTS:
        block = back_ref[:, low:high]
        left = iter(outs)
        for run in chosen:
            first, last = PIECES[run[0]], PIECES[run[-1] + 1]
            part = jnp.dot(mix_ref[first:last, :SLOTS], block, preferred_element_type=F32)
            part = part + jnp.dot(mix_ref[first:last, SLOTS:], block, preferred_element_type=F32)
            part = part.astype(BF16)
            for k in run:
                next(left)[:, low:high] = part[PIECES[k] - first : PIECES[k + 1] - first]


def combine_some(mix, back, chosen):
    shapes = [PIECE_SHAPES[k] for run in chosen for k in run]
    return pl.pallas_call(
        functools.partial(combine_kernel, chosen),
        grid=(1,),
        in_specs=[whole(mix.shape), whole(back.shape)],
        out_specs=[whole(shape) for shape in shapes],
        out_shape=[jax.ShapeDtypeStruct(shape, BF16) for shape in shapes],
        compiler_params=params(1),
        name="combine",
    )(mix, back)


def combine(mix, back):
    middle = combine_some(mix, back, ((3, 4, 5, 6),))
    rest = combine_some(mix, back, ((0, 1, 2), (7, 8)))
    return [*rest[:3], *middle, *rest[3:]]


def finish_kernel(hidden_ref, *refs):
    parts, out_ref = refs[:5], refs[5]
    total = parts[0][...].astype(F32)
    for part in parts[1:]:
        total = total + part[...].astype(F32)
    out_ref[...] = (hidden_ref[...] + total).astype(BF16)


def finish(hidden, parts):
    return pl.pallas_call(
        finish_kernel,
        grid=(1,),
        in_specs=[whole((CHUNK, WIDTH))] * 6,
        out_specs=whole((CHUNK, WIDTH)),
        out_shape=jax.ShapeDtypeStruct((CHUNK, WIDTH), BF16),
        compiler_params=params(1),
        name="finish",
    )(hidden, *parts)


def pack_kernel(_, up_ref, down_ref, out_ref):
    double, units = up_ref.shape[1], down_ref.shape[0]
    pad = jnp.zeros((UP_ROWS - double, WIDTH), BF16)
    out_ref[:UP_ROWS, :] = jnp.concatenate([up_ref[0], pad])
    pad = jnp.zeros((UNITS - units, WIDTH), BF16)
    out_ref[UP_ROWS:, :] = jnp.concatenate([down_ref[...], pad])


def pack(local, ups, down):
    shape = (UP_ROWS + UNITS, WIDTH)
    return pl.pallas_call(
        pack_kernel,
        grid_spec=pltpu.PrefetchScalarGridSpec(
            num_scalar_prefetch=1,
            grid=(1,),
            in_specs=[
                pl.BlockSpec((1, *ups.shape[1:]), lambda i, local: (local[0], 0, 0)),
                pl.BlockSpec(down.shape, lambda i, local: (0, 0)),
            ],
            out_specs=pl.BlockSpec(shape, lambda i, local: (0, 0)),
        ),
        out_shape=jax.ShapeDtypeStruct(shape, BF16),
        compiler_params=params(1),
        name="pack",
    )(local, ups, down)


def activation(x, rows, units):
    shape = (rows.shape[0], units)
    row = lax.broadcasted_iota(jnp.int32, shape, 0)
    col = lax.broadcasted_iota(jnp.int32, shape, 1)
    pick = jnp.where(row == 2 * col, 1.0, 0.0).astype(BF16)
    both = scores_of(x, rows)
    up = jnp.concatenate([both[:, 1:], both[:, :1]], axis=1)
    act = ((up + 1.0) * both * jax.nn.sigmoid(1.702 * both)).astype(BF16)
    return jnp.dot(act, pick, preferred_element_type=F32).astype(BF16)


def open_kernel(x_ref, up_ref, down_ref, out_ref):
    act = activation(x_ref[:, :WIDTH], up_ref[...], down_ref.shape[0])
    for low, high in COLUMN_CUTS:
        part = jnp.dot(act, down_ref[:, low:high], preferred_element_type=F32)
        out_ref[:, low:high] = part.astype(BF16)


def close_kernel(x_ref, half_ref, piece_ref, out_ref):
    act = activation(x_ref[:, :WIDTH], piece_ref[:UP_ROWS, :], UNITS)
    for low, high in COLUMN_CUTS:
        total = half_ref[:, low:high].astype(F32)
        total = total + jnp.dot(
            act, piece_ref[UP_ROWS:, low:high], preferred_element_type=F32
        )
        out_ref[:, low:high] = total.astype(out_ref.dtype)


def expert_cost(rows, flops):
    return pl.CostEstimate(
        flops=rows * flops, bytes_accessed=6 << 20, transcendentals=rows * 360
    )


def open_experts(x, up, down):
    shape = (x.shape[0], WIDE)
    return pl.pallas_call(
        open_kernel,
        grid=(1,),
        in_specs=[whole(x.shape), whole(up.shape), whole(down.shape)],
        out_specs=whole(shape),
        out_shape=jax.ShapeDtypeStruct(shape, BF16),
        compiler_params=params(1),
        cost_estimate=expert_cost(shape[0], WIDTH * 720),
        name="open_experts",
    )(x, up, down)


def close_experts(x, act, piece):
    rows = x.shape[0]
    return pl.pallas_call(
        close_kernel,
        grid=(1,),
        in_specs=[whole(w.shape) for w in (x, act, piece)],
        out_specs=whole((rows, WIDE)),
        out_shape=jax.ShapeDtypeStruct((rows, WIDE), BF16),
        compiler_params=params(1),
        cost_estimate=expert_cost(rows, WIDTH * 1440),
        name="close_experts",
    )(x, act, piece)


MOVES = (
    ((0, 8), (1, 0), (7, 9), (2, 1), (10, 2), (11, 10), (9, 3), (12, 11))
    + ((5, 12), (3, 4), (6, 13), (4, 5), (8, 6), (13, 14), (15, 7), (14, 15)),
    ((7, 8), (2, 0), (1, 9), (0, 1), (9, 2), (12, 10), (11, 3), (10, 11))
    + ((4, 12), (6, 4), (5, 13), (3, 5), (14, 6), (15, 14), (13, 7), (8, 15)),
)
SENT = tuple(sum((goal % 2) << source for source, goal in moves) for moves in MOVES)


def shift(step):
    return [(i, (i + step) % 8) for i in range(8)]


def tie(*values):
    return lax.optimization_barrier(values)


def add(a, b):
    return (a.astype(F32) + b.astype(F32)).astype(BF16)


def move(chunk, step):
    return lax.ppermute(chunk, "expert", shift(step))


def join_kernel(*refs):
    for side in range(2):
        own, whole_ref, half, out = refs[3 * side : 3 * side + 3] + (refs[6 + side],)
        rows = slice(side * CHUNK // 2, (side + 1) * CHUNK // 2)
        rest = slice((1 - side) * CHUNK // 2, (2 - side) * CHUNK // 2)
        total = own[...].astype(F32) + whole_ref[...].astype(F32)
        out[rest, :] = total[rest].astype(BF16)
        out[rows, :] = (total[rows] + half[...].astype(F32)).astype(BF16)


def join(*parts):
    return pl.pallas_call(
        join_kernel,
        grid=(1,),
        in_specs=[whole(part.shape) for part in parts],
        out_specs=[whole((CHUNK, WIDTH))] * 2,
        out_shape=[jax.ShapeDtypeStruct((CHUNK, WIDTH), BF16)] * 2,
        compiler_params=params(1),
        name="join",
    )(*parts)


def sum_to_owner(parts, beside=None):
    own, up_1, up_2, up_3, half_down, half_up, down_3, down_2, down_1 = parts
    down, up = join(
        down_2, move(down_3, -1), move(half_down, -2), up_2, move(up_3, 1), move(half_up, 2)
    )
    if beside is not None:
        beside, down, up = tie(beside, down, up)
    return beside, [own, move(down_1, -1), move(up_1, 1), move(down, -2), move(up, 2)]


def gather(mine, beside):
    near = move(mine, -1), move(mine, 1)
    *beside, after, before = tie(*beside, move(mine, -2), move(mine, 2))
    half = CHUNK // 2
    far = move(after[:half], -2), move(before[half:], 2)
    third, fifth = move(after, -1), move(before, 1)
    return beside, [mine, near[0], after, third, *far, fifth, before, near[1]]


SWAP = [(0, 1), (1, 0)]


def shards(
    residual,
    queries,
    response_key_value,
    prompt_cache,
    lengths,
    out_proj,
    norm_gain,
    gate_up,
    down_proj,
    expert_ids,
    gate_weights,
):
    z = lax.axis_index("expert")
    core = lax.axis_index("core")
    place = z.astype(jnp.int32).reshape(1)

    own = prompt_cache.reshape(prompt_cache.shape[1], 2 * HEAD)
    near = lax.ppermute(own, "core", SWAP)
    far = lax.ppermute(own, "xh", SWAP)

    gate_up = jnp.transpose(gate_up, (0, 2, 1))
    device = core * 8 + z
    chosen = [
        lax.bitwise_and(lax.shift_right_logical(jnp.int32(table), device), 1) for table in SENT
    ]

    def send_weights(piece, n):
        return lax.ppermute(piece, ("core", "expert"), MOVES[n])

    def pick(array, n):
        return lax.dynamic_index_in_dim(array, chosen[n], 0, keepdims=False)

    up, near = tie(pick(gate_up, 0), near)
    up_first = send_weights(up, 0)
    response = response_key_value.reshape(ROWS, 2 * HEAD)
    top, total = attend_near(lengths, queries, response, own, near)

    down, far, top = tie(pick(down_proj, 0), far, top)
    down_first = send_weights(down, 0)
    far_near = lax.ppermute(far, "core", SWAP)
    partial = attend_far(place, queries, far, far_near, top, total, out_proj.T)
    up_first, *partial = tie(up_first, *partial)

    ids, weights, residual, partial[0] = tie(
        expert_ids.T, gate_weights.T, residual.T, partial[0]
    )
    send, mix = routing(place, ids, weights)
    residual = own_rows(place, residual)
    down_first, partial = sum_to_owner(partial, down_first)
    hidden, normed = norm(residual, norm_gain.reshape(1, WIDTH), partial)

    gate_up, down_proj, normed = tie(gate_up, down_proj, normed)
    piece = pack(chosen[1].reshape(1), gate_up, pick(down_proj, 1))
    (piece, send, mix), gathered = gather(normed, (piece, send, mix))
    outgoing = dispatch(send, gathered)
    second = send_weights(piece, 1)
    mine = lax.all_to_all(outgoing, ("prompt", "xh"), split_axis=0, concat_axis=0, tiled=True)
    other = lax.ppermute(mine, "core", SWAP)
    act_mine = open_experts(mine, up_first, down_first)
    act_other = open_experts(other, up_first, down_first)
    second, act_mine, act_other = tie(second, act_mine, act_other)
    done_other = close_experts(other, act_other, second)
    done_mine = close_experts(mine, act_mine, second)
    done = add(done_mine, lax.ppermute(done_other, "core", SWAP))
    back = lax.all_to_all(done, ("prompt", "xh"), split_axis=0, concat_axis=0, tiled=True)
    return finish(hidden, sum_to_owner(combine(mix, back))[1])


def solution(mesh):
    fine = Mesh(mesh.devices.reshape(8, 2, 2, 8), ("prompt", "xh", "core", "expert"))
    sample = ("prompt", "xh", "core")
    placed = (
        P(sample, None),
        P(sample, "expert"),
        P(sample, "expert", None),
        P("prompt", ("xh", "core"), "expert", None),
        P(sample),
        P("expert", None),
        P(),
        P(sample, None, "expert"),
        P(sample, "expert", None),
        P(sample, None),
        P(sample, None),
    )
    return jax.shard_map(
        shards,
        mesh=fine,
        in_specs=placed,
        out_specs=P((*sample, "expert"), None),
        check_vma=False,
    )
```
